256 devices in a mesh: leaf: 16 (over z, core), front: 16 (over y, x).
Axes of the slice: x: 4, y: 4, z: 8, core: 2. Of those that a mesh axis runs over, the one named last changes fastest.
Arguments:
- leaf_source: float32 [16, 2048, 128], P('leaf', 'front'), may hold values from -6 to 6
- top_source: float32 [7, 512, 128], P(None, 'front'), may hold values from -6 to 6
- leaf_lower_inverse: bfloat16 [16, 2048, 2048], P('leaf', 'front'), as said below
- leaf_upper_inverse: bfloat16 [16, 2048, 2048], P('leaf', 'front'), as said below
- leaf_lower_block: bfloat16 [16, 1024, 2048], P('leaf', None, 'front'), may hold values from -0.09375 to 0.09375
- leaf_upper_block: bfloat16 [16, 2048, 1024], P('leaf', 'front'), may hold values from -0.1875 to 0.1875
- top_lower_inverse: bfloat16 [7, 512, 512], P(None, 'front'), as said below
- top_upper_inverse: bfloat16 [7, 512, 512], P(None, 'front'), as said below
- top_lower_block: bfloat16 [6, 512, 512], P(None, None, 'front'), may hold values from -0.25 to 0.25
- top_upper_block: bfloat16 [6, 512, 512], P(None, 'front'), may hold values from -0.25 to 0.25
- leaf_targets: int32 [16, 1024], P('leaf'), may hold values from 0 to 3583, as said below
- top_targets: int32 [6, 512], replicated, may hold values from 0 to 1535, as said below
Outputs:
- leaf_solution: float32 [16, 2048, 128], P('leaf', 'front')
- top_solution: float32 [7, 512, 128], P(None, 'front')
The draws below stay inside these ranges and needn't reach their ends.
Inputs may be any that keep to these rules, and one draw needn't show every extreme that they name: `leaf_targets`: each update row of leaf l lands in one of its 3 ancestors: the separator of height h above leaf l has index 2**(h-1) - 1 + l * 2**(h-1) // 16. Rows may repeat. `top_targets`: each update row of separator s + 1 lands in a row of one of its ancestors in the binary tree of separators (the parent of separator s + 1 is separator (s + 1 - 1) // 2). Rows may repeat. `leaf_lower_inverse`: each block is the identity plus independent entries of deviation 0.6 / sqrt(2048). `leaf_upper_inverse`: as leaf_lower_inverse. `top_lower_inverse`: each block is the identity plus independent entries of deviation 0.6 / sqrt(512). `top_upper_inverse`: as top_lower_inverse.
All inputs are finite; a program needn't handle non-finite values.
Results may differ from the reference program's by a relative error of at most 0.022.
Values may be sent and summed in bfloat16 or wider, within the bound.
No kernel may reach another device: no remote copies, remote signals or barrier semaphores. Data moves between devices by JAX's collectives and lax.ppermute only.
A program may use at most 64 MiB of HBM per device.

```python
import math
import jax
import jax.numpy as jnp
import numpy as np
from jax import lax

SUB = 2048
SEP = 512
UPD = 1024
TUPD = 512
RHS = 128
LEVELS = 3
NSEP = 7
LEAVES = 16


def near_identity(noise, order):
    return jnp.eye(order, dtype=jnp.float32) + noise * (0.6 / math.sqrt(order))


def draw_leaf_lower_inverse(key, part):
    key = jax.random.fold_in(key, 11)
    noise = jax.random.normal(key, (LEAVES, SUB, SUB), jnp.float32)
    return near_identity(noise, SUB).astype(jnp.bfloat16)


def draw_leaf_upper_inverse(key, part):
    key = jax.random.fold_in(key, 13)
    noise = jax.random.normal(key, (LEAVES, SUB, SUB), jnp.float32)
    return near_identity(noise, SUB).astype(jnp.bfloat16)


def draw_top_lower_inverse(key, part):
    key = jax.random.fold_in(key, 17)
    noise = jax.random.normal(key, (NSEP, SEP, SEP), jnp.float32)
    return near_identity(noise, SEP).astype(jnp.bfloat16)


def draw_top_upper_inverse(key, part):
    key = jax.random.fold_in(key, 19)
    noise = jax.random.normal(key, (NSEP, SEP, SEP), jnp.float32)
    return near_identity(noise, SEP).astype(jnp.bfloat16)


def draw_leaf_targets(key, part):
    key = jax.random.fold_in(key, 31)
    pick_key, offset_key = jax.random.split(key)
    height = jax.random.randint(pick_key, (LEAVES, UPD), 0, LEVELS)
    spread = jnp.left_shift(jnp.int32(1), height)
    leaf_index = jnp.arange(LEAVES, dtype=jnp.int32)[:, None]
    owner = spread - 1 + leaf_index * spread // LEAVES
    offset = jax.random.randint(offset_key, (LEAVES, UPD), 0, SEP)
    targets = (owner * SEP + offset).astype(jnp.int32)
    targets = targets.at[0, 0].set(0)
    targets = targets.at[LEAVES - 1, UPD - 1].set(NSEP * SEP - 1)
    return targets


def draw_top_targets(key, part):
    key = jax.random.fold_in(key, 37)
    pick_key, offset_key = jax.random.split(key)
    own_table = np.floor(np.log2(np.arange(2, NSEP + 1))).astype(np.int32)
    own_height = jnp.asarray(own_table)[:, None]
    position = jnp.arange(2, NSEP + 1, dtype=jnp.int32)[:, None] - jnp.left_shift(jnp.int32(1), own_height)
    ancestor_height = jax.random.randint(pick_key, (NSEP - 1, TUPD), 0, own_height)
    ancestor = jnp.left_shift(jnp.int32(1), ancestor_height) - 1 + jnp.right_shift(position, own_height - ancestor_height)
    offset = jax.random.randint(offset_key, (NSEP - 1, TUPD), 0, SEP)
    targets = (ancestor * SEP + offset).astype(jnp.int32)
    targets = targets.at[0, 0].set(0)
    targets = targets.at[NSEP - 2, TUPD - 1].set(NSEP // 2 * SEP - 1)
    return targets


def levels(key, extent, cuts, least, top_value):
    gain, own = 1.0, jax.random.fold_in(key, 6)
    for dim, parts in cuts:
        heights = jnp.exp(jax.random.uniform(jax.random.fold_in(own, dim), (parts,), jnp.float32, least / len(cuts), top_value / len(cuts)))
        gain = gain * jnp.repeat(heights, extent[dim] // parts).reshape([-1 if axis == dim else 1 for axis in range(len(extent))])
    return gain


def bell_draw(stream_key, extent, scale, most, shards=(), kind=jnp.bfloat16):
    values = scale * jax.random.normal(stream_key, extent, jnp.float32)
    if shards:
        values = values * levels(stream_key, extent, shards, -0.22, 0.18)
    return jnp.clip(values, -most, most).astype(kind)


def setup_inputs(seed: int = 0) -> dict:
    key_of = jax.random.split(jax.random.key(seed), 13)
    leaf_source = bell_draw(key_of[0], (LEAVES, SUB, RHS), 1.0, 6.0, ((0, 16), (1, 16)), jnp.float32)
    top_source = bell_draw(key_of[1], (NSEP, SEP, RHS), 1.0, 6.0, ((1, 16),), jnp.float32)
    leaf_lower_inverse = draw_leaf_lower_inverse(jax.random.fold_in(key_of[12], 71), 0)
    leaf_upper_inverse = draw_leaf_upper_inverse(jax.random.fold_in(key_of[12], 71), 0)
    leaf_lower_block = bell_draw(key_of[4], (LEAVES, UPD, SUB), (SUB * LEAVES // 8) ** -0.5, 0.09375, ((0, 16), (2, 16)))
    leaf_upper_block = bell_draw(key_of[5], (LEAVES, SUB, UPD), UPD ** -0.5, 0.1875, ((0, 16), (1, 16)))
    top_lower_inverse = draw_top_lower_inverse(jax.random.fold_in(key_of[12], 71), 0)
    top_upper_inverse = draw_top_upper_inverse(jax.random.fold_in(key_of[12], 71), 0)
    top_lower_block = bell_draw(key_of[8], (NSEP - 1, TUPD, SEP), SEP ** -0.5, 0.25, ((2, 16),))
    top_upper_block = bell_draw(key_of[9], (NSEP - 1, SEP, TUPD), TUPD ** -0.5, 0.25, ((1, 16),))
    leaf_targets = draw_leaf_targets(jax.random.fold_in(key_of[12], 71), 0)
    top_targets = draw_top_targets(jax.random.fold_in(key_of[12], 71), 0)
    return {"leaf_source": leaf_source, "top_source": top_source, "leaf_lower_inverse": leaf_lower_inverse, "leaf_upper_inverse": leaf_upper_inverse, "leaf_lower_block": leaf_lower_block, "leaf_upper_block": leaf_upper_block, "top_lower_inverse": top_lower_inverse, "top_upper_inverse": top_upper_inverse, "top_lower_block": top_lower_block, "top_upper_block": top_upper_block, "leaf_targets": leaf_targets, "top_targets": top_targets}


def rounded(value):
    return lax.optimization_barrier(value.astype(jnp.bfloat16)).astype(jnp.float32)


def reference(leaf_source, top_source, leaf_lower_inverse, leaf_upper_inverse, leaf_lower_block, leaf_upper_block, top_lower_inverse, top_upper_inverse, top_lower_block, top_upper_block, leaf_targets, top_targets):
    rows_all = NSEP * SEP

    def leaf_forward(carry, inputs):
        source, inverse, block, targets = inputs
        solved = jnp.dot(inverse, source.astype(jnp.bfloat16), preferred_element_type=jnp.float32)
        update = jnp.dot(block, solved.astype(jnp.bfloat16), preferred_element_type=jnp.float32)
        return carry.at[targets].add(update), solved

    start_sum = jnp.zeros((rows_all, RHS), jnp.float32)
    gathered, leaf_solved = lax.scan(leaf_forward, start_sum, (leaf_source, leaf_lower_inverse, leaf_lower_block, leaf_targets))
    target = top_source.reshape(rows_all, RHS) - gathered
    forward_solved = {}
    for height in range(LEVELS, 0, -1):
        first = 2 ** (height - 1) - 1
        last = 2 ** height - 1
        block_source = rounded(target[first * SEP:last * SEP].reshape(last - first, SEP, RHS))
        solved = jnp.einsum("sij,sjc->sic", top_lower_inverse[first:last].astype(jnp.float32), block_source)
        forward_solved[height] = solved
        if height > 1:
            update = jnp.einsum("suj,sjc->suc", top_lower_block[first - 1:last - 1].astype(jnp.float32), rounded(solved))
            target = target.at[top_targets[first - 1:last - 1].reshape(-1)].add(-update.reshape(-1, RHS))
    solution = jnp.zeros((NSEP, SEP, RHS), jnp.float32)
    solution_round = jnp.zeros((rows_all, RHS), jnp.bfloat16)
    for height in range(1, LEVELS + 1):
        first = 2 ** (height - 1) - 1
        last = 2 ** height - 1
        residue = forward_solved[height]
        if height > 1:
            picked = solution_round[top_targets[first - 1:last - 1]].astype(jnp.float32)
            residue = residue - jnp.einsum("sju,suc->sjc", top_upper_block[first - 1:last - 1].astype(jnp.float32), picked)
        solved = jnp.einsum("sij,sjc->sic", top_upper_inverse[first:last].astype(jnp.float32), rounded(residue))
        solution = solution.at[first:last].set(solved)
        solution_round = solution_round.at[first * SEP:last * SEP].set(solved.astype(jnp.bfloat16).reshape(-1, RHS))

    def leaf_backward(inputs):
        solved, inverse, block, targets = inputs
        residue = solved - jnp.dot(block, solution_round[targets], preferred_element_type=jnp.float32)
        return jnp.dot(inverse, residue.astype(jnp.bfloat16), preferred_element_type=jnp.float32)

    leaf_solution = lax.map(leaf_backward, (leaf_solved, leaf_upper_inverse, leaf_upper_block, leaf_targets))
    return leaf_solution, solution
```

```python
import jax
import jax.numpy as jnp
from jax import lax
from jax.experimental import pallas as pl
from jax.experimental.pallas import tpu as pltpu
from jax.sharding import PartitionSpec as P

BF = jnp.bfloat16
F32 = jnp.float32
FRONT = 16
LEAVES = 16
SUB = 2048
SEP = 512
UPD = 1024
RHS = 128
ROWS = SEP // FRONT
SPAN = 3 * SEP
HALF = SPAN // 2
PIECE = SUB // FRONT
NT = (((1,), (1,)), ((), ()))
NN = (((1,), (0,)), ((), ()))


def dot(a, b, dims):
    return lax.dot_general(a, b, dims, preferred_element_type=F32)


def split_dot(x, w, dims):
    head = x.astype(BF).astype(F32)
    both = jnp.concatenate([head, x - head], axis=0).astype(BF)
    out = dot(both, w, dims)
    return out[:8] + out[8:]


def fold(x):
    return jnp.concatenate([x[:, :HALF], x[:, HALF:]], axis=0)


def unfold(x):
    return jnp.concatenate([x[:8], x[8:]], axis=1)


def one_hot(first, count, places):
    rows = lax.broadcasted_iota(jnp.int32, (count, places.shape[1]), 0) + first
    return jnp.where(rows == places, 1.0, 0.0).astype(BF)


def leaf_places(targets):
    owner = targets >> 9
    height = jnp.where(owner > 0, 1, 0) + jnp.where(owner > 2, 1, 0)
    return (height << 9) | (targets & (SEP - 1))


def ancestor_places(targets):
    return jnp.where(targets >= SEP, SEP, 0) + (targets & (SEP - 1))


def prepare_kernel(source, low_inv, up_inv, low, up, send, later):
    leaf = lax.axis_index("leaf")
    third = 3 + (leaf >> 2)
    second = 1 + (leaf >> 3)
    piece = source[0].astype(BF)
    wide = jnp.concatenate([piece[q * 32 : q * 32 + 32] for q in range(4)], axis=1)
    for to in range(FRONT):
        send[to, 0:32, :] = wide

    @pl.when((leaf & 1) == 0)
    def _():
        a = low_inv[third]
        b = low_inv[second]
        for to in range(FRONT):
            send[to, 32:64, :] = a
            send[to, 64:96, :] = b

    @pl.when((leaf & 1) == 1)
    def _():
        a = low[third - 1].astype(F32).T.astype(BF)
        b = low[second - 1].astype(F32).T.astype(BF)
        for to in range(FRONT):
            send[to, 32:64, :] = a
            send[to, 64:96, :] = b

    later[0:32, :] = low_inv[0]
    later[32:64, :] = up_inv[0]
    later[64:96, :] = up[second - 1]
    later[96:128, :] = up_inv[second]
    later[128:160, :] = up[third - 1]
    later[160:192, :] = up_inv[third]


def leaf_forward_kernel(got, inverse, block, targets, top, solved_out, send, source):
    leaf = lax.axis_index("leaf")
    front = lax.axis_index("front")
    for k in range(FRONT):
        for q in range(4):
            source[k * PIECE + q * 32 : k * PIECE + q * 32 + 32, :] = got[k, 0:32, q * RHS : q * RHS + RHS]
    solved = dot(inverse[0], source[...], NN)
    solved_out[...] = solved
    turned = solved.T.astype(BF)
    update = dot(turned, block[0], NT)
    own = jnp.concatenate(
        [
            top[0] * (1 / 16),
            top[1 + (leaf >> 3)] * (1 / 8),
            top[3 + (leaf >> 2)] * (1 / 4),
            jnp.zeros((32, RHS), F32),
        ],
        axis=0,
    ).T
    lhs = jnp.concatenate([-update, own], axis=1).astype(BF)
    lane = lax.broadcasted_iota(jnp.int32, (1, RHS), 1)
    top_places = jnp.where(lane < 96, ((lane >> 5) << 9) + front * ROWS + (lane & 31), -1)
    places = jnp.concatenate([leaf_places(targets[...]), top_places], axis=1)
    low = dot(lhs, one_hot(0, HALF, places), NT)
    high = dot(lhs, one_hot(HALF, HALF, places), NT)
    for to in range(FRONT):
        send[to] = jnp.concatenate([low[to * 8 : to * 8 + 8], high[to * 8 : to * 8 + 8]], axis=0).astype(BF)


def top_forward_kernel(got, first, swapped, targets, send, mats):
    leaf = lax.axis_index("leaf")

    @pl.when((leaf & 1) == 0)
    def _():
        mats[0] = first[:, 32:64, :].reshape(SEP, SEP)
        mats[1] = first[:, 64:96, :].reshape(SEP, SEP)
        mats[2] = swapped[:, 32:64, :].reshape(SEP, SEP)
        mats[3] = swapped[:, 64:96, :].reshape(SEP, SEP)

    @pl.when((leaf & 1) == 1)
    def _():
        mats[0] = swapped[:, 32:64, :].reshape(SEP, SEP)
        mats[1] = swapped[:, 64:96, :].reshape(SEP, SEP)
        mats[2] = first[:, 32:64, :].reshape(SEP, SEP)
        mats[3] = first[:, 64:96, :].reshape(SEP, SEP)

    total = got[0].astype(F32)
    for k in range(1, FRONT):
        total = total + got[k].astype(F32)
    total = unfold(total)
    target1 = total[:, :SEP]
    target2 = total[:, SEP : 2 * SEP]
    target3 = total[:, 2 * SEP :]
    solved3 = split_dot(target3, mats[0], NT)
    update3 = split_dot(solved3, mats[2], NN)
    places3 = ancestor_places(targets[pl.ds(2 + (leaf >> 2), 1), :])
    spread3 = split_dot(update3, one_hot(0, 2 * SEP, places3), NT)
    target1 = target1 - spread3[:, :SEP]
    target2 = target2 - spread3[:, SEP:]
    solved2 = split_dot(target2, mats[1], NT)
    update2 = split_dot(solved2, mats[3], NN)
    places2 = targets[pl.ds(leaf >> 3, 1), :]
    target1 = target1 - split_dot(update2, one_hot(0, SEP, places2), NT)
    out = fold(jnp.concatenate([target1, solved2, solved3], axis=1)).astype(BF)
    for to in range(LEAVES):
        send[to] = out


def top_backward_kernel(got, later, targets, send):
    leaf = lax.axis_index("leaf")
    total1 = jnp.zeros((8, SEP), F32)
    total2 = jnp.zeros((8, SEP), F32)
    total3 = jnp.zeros((8, SEP), F32)
    for k in range(LEAVES):
        part = unfold(got[k].astype(F32))
        total1 = total1 + part[:, :SEP]
        total2 = total2 + part[:, SEP : 2 * SEP] * jnp.where((leaf >> 3) == (k >> 3), 1.0, 0.0)
        total3 = total3 + part[:, 2 * SEP :] * jnp.where((leaf >> 2) == (k >> 2), 1.0, 0.0)

    def mat(i):
        return later[:, i * 32 : i * 32 + 32, :].reshape(SEP, SEP)

    x1 = split_dot(split_dot(total1, mat(0), NT), mat(1), NT)
    places2 = targets[pl.ds(leaf >> 3, 1), :]
    picked2 = split_dot(x1, one_hot(0, SEP, places2), NN)
    x2 = split_dot(total2 - split_dot(picked2, mat(2), NT), mat(3), NT)
    places3 = ancestor_places(targets[pl.ds(2 + (leaf >> 2), 1), :])
    picked3 = split_dot(jnp.concatenate([x1, x2], axis=1), one_hot(0, 2 * SEP, places3), NN)
    x3 = split_dot(total3 - split_dot(picked3, mat(4), NT), mat(5), NT)
    out = fold(jnp.concatenate([x1, x2, x3], axis=1)).astype(BF)
    for to in range(FRONT):
        send[to] = out


def leaf_backward_kernel(got, solved, block, targets, send, own):
    front = lax.axis_index("front")
    full = jnp.concatenate([unfold(got[k].astype(F32)) for k in range(FRONT)], axis=0).astype(BF)
    picked = dot(full, one_hot(0, SPAN, leaf_places(targets[...])), NN).astype(BF)
    residue = (solved[...] - dot(block[0], picked, NT)).astype(BF)
    for to in range(FRONT):
        send[to] = residue
    row = lax.broadcasted_iota(jnp.int32, (96, SPAN), 0)
    column = lax.broadcasted_iota(jnp.int32, (96, SPAN), 1)
    pick = jnp.where(column == ((row >> 5) << 9) + front * ROWS + (row & 31), 1.0, 0.0).astype(BF)
    own[...] = dot(pick, full, NT).astype(BF)


def finish_kernel(got, inverse, own, near, far, other, leaf_out, top_out):
    leaf = lax.axis_index("leaf")
    leaf_out[0] = dot(inverse[0], got[...].reshape(SUB, RHS), NN)
    second = leaf >> 3
    third = leaf >> 2
    top_out[0] = own[0:32, :].astype(F32)
    top_out[1 + second] = own[32:64, :].astype(F32)
    top_out[1 + (second ^ 1)] = far[32:64, :].astype(F32)
    top_out[3 + third] = own[64:96, :].astype(F32)
    top_out[3 + (third ^ 1)] = near[64:96, :].astype(F32)
    top_out[3 + (third ^ 2)] = far[64:96, :].astype(F32)
    top_out[3 + (third ^ 3)] = other[64:96, :].astype(F32)


def call(kernel, outs, args, scratch=(), flops=0, size=0):
    shapes = [jax.ShapeDtypeStruct(shape, kind) for shape, kind in outs]
    return pl.pallas_call(
        kernel,
        out_shape=shapes,
        in_specs=[pl.BlockSpec(memory_space=pltpu.VMEM)] * len(args),
        out_specs=[pl.BlockSpec(memory_space=pltpu.VMEM)] * len(shapes),
        scratch_shapes=list(scratch),
        compiler_params=pltpu.CompilerParams(vmem_limit_bytes=32 * 1024 * 1024),
        cost_estimate=pl.CostEstimate(flops=flops, bytes_accessed=size, transcendentals=0),
    )(*args)


def swap(x, flip):
    return lax.ppermute(x, "leaf", [(i, i ^ flip) for i in range(LEAVES)])


def exchange(x, axis):
    return lax.all_to_all(x, axis, 0, 0, tiled=True)


def body(
    leaf_source,
    top_source,
    leaf_lower_inverse,
    leaf_upper_inverse,
    leaf_lower_block,
    leaf_upper_block,
    top_lower_inverse,
    top_upper_inverse,
    top_lower_block,
    top_upper_block,
    leaf_targets,
    top_targets,
):
    send, later = call(
        prepare_kernel,
        [((FRONT, 96, SEP), BF), ((192, SEP), BF)],
        (leaf_source, top_lower_inverse, top_upper_inverse, top_lower_block, top_upper_block),
        size=3 << 20,
    )
    later = lax.all_gather(later, "front", axis=0, tiled=False)
    first = exchange(send, "front")
    swapped = swap(first, 1)
    solved, send = call(
        leaf_forward_kernel,
        [((PIECE, RHS), F32), ((FRONT, 16, HALF), BF)],
        (first, leaf_lower_inverse, leaf_lower_block, leaf_targets, top_source),
        scratch=[pltpu.VMEM((SUB, RHS), BF)],
        flops=2 * RHS * (PIECE * SUB + UPD * PIECE + UPD * SPAN),
        size=4 << 20,
    )
    got = exchange(send, "front")
    (send,) = call(
        top_forward_kernel,
        [((LEAVES, 16, HALF), BF)],
        (got, first, swapped, top_targets),
        scratch=[pltpu.VMEM((4, SEP, SEP), BF)],
        flops=2 * 256 * SEP * SEP * 8,
        size=4 << 20,
    )
    got = exchange(send, "leaf")
    (send,) = call(
        top_backward_kernel,
        [((FRONT, 16, HALF), BF)],
        (got, later, top_targets),
        flops=2 * 256 * SEP * SEP * 9,
        size=5 << 20,
    )
    got = exchange(send, "front")
    send, own = call(
        leaf_backward_kernel,
        [((FRONT, PIECE, RHS), BF), ((96, RHS), BF)],
        (got, solved, leaf_upper_block, leaf_targets),
        flops=2 * RHS * (UPD * SPAN + UPD * PIECE),
        size=2 << 20,
    )
    near, far, other = swap(own, 4), swap(own, 8), swap(own, 12)
    got = exchange(send, "front")
    leaf_solution, top_solution = call(
        finish_kernel,
        [((1, PIECE, RHS), F32), ((7, ROWS, RHS), F32)],
        (got, leaf_upper_inverse, own, near, far, other),
        flops=2 * RHS * PIECE * SUB,
        size=2 << 20,
    )
    return leaf_solution, top_solution


def solution(mesh):
    in_specs = (
        P("leaf", "front", None),
        P(None, "front", None),
        P("leaf", "front", None),
        P("leaf", "front", None),
        P("leaf", None, "front"),
        P("leaf", "front", None),
        P(None, "front", None),
        P(None, "front", None),
        P(None, None, "front"),
        P(None, "front", None),
        P("leaf", None),
        P(),
    )
    out_specs = (P("leaf", "front", None), P(None, "front", None))
    return jax.shard_map(body, mesh=mesh, in_specs=in_specs, out_specs=out_specs, check_vma=False)
```

```python
import jax
import jax.numpy as jnp
from jax import lax
from jax.experimental import pallas as pl
from jax.experimental.pallas import tpu as pltpu
from jax.sharding import PartitionSpec as P

BF = jnp.bfloat16
F32 = jnp.float32
FRONT = 16
LEAVES = 16
SUB = 2048
SEP = 512
UPD = 1024
RHS = 128
ROWS = SEP // FRONT
SPAN = 3 * SEP
HALF = SPAN // 2
PIECE = SUB // FRONT
NT = (((1,), (1,)), ((), ()))
NN = (((1,), (0,)), ((), ()))


def dot(a, b, dims):
    return lax.dot_general(a, b, dims, preferred_element_type=F32)


def split_dot(x, w, dims):
    head = x.astype(BF).astype(F32)
    both = jnp.concatenate([head, x - head], axis=0).astype(BF)
    out = dot(both, w, dims)
    return out[:8] + out[8:]


def fold(x):
    return jnp.concatenate([x[:, :HALF], x[:, HALF:]], axis=0)


def unfold(x):
    return jnp.concatenate([x[:8], x[8:]], axis=1)


def one_hot(first, count, places):
    rows = lax.broadcasted_iota(jnp.int32, (count, places.shape[1]), 0) + first
    return jnp.where(rows == places, 1.0, 0.0).astype(BF)


def leaf_places(targets):
    owner = targets >> 9
    height = jnp.where(owner > 0, 1, 0) + jnp.where(owner > 2, 1, 0)
    return (height << 9) | (targets & (SEP - 1))


def ancestor_places(targets):
    return jnp.where(targets >= SEP, SEP, 0) + (targets & (SEP - 1))


def prepare_kernel(source, low_inv, up_inv, low, up, send, later, piece, held, sems):
    leaf = lax.axis_index("leaf")
    third = 3 + (leaf >> 2)
    second = 1 + (leaf >> 3)
    role = leaf & 3
    core = leaf & 1

    def fetch(ref, index, slot):
        return pltpu.make_async_copy(ref.at[index], held.at[slot], sems.at[slot])

    start = pltpu.make_async_copy(source.at[0], piece, sems.at[4])
    start.start()

    @pl.when(core == 0)
    def _():
        fetch(low_inv, jnp.where(role == 0, third, second), 0).start()
        fetch(low_inv, 0, 1).start()
        fetch(up_inv, 0, 2).start()
        fetch(up, second - 1, 3).start()

    @pl.when(core == 1)
    def _():
        fetch(low, jnp.where(role == 1, third, second) - 1, 0).start()
        fetch(up_inv, second, 1).start()
        fetch(up, third - 1, 2).start()
        fetch(up_inv, third, 3).start()

    for slot in range(1, 4):
        fetch(low_inv, 0, slot).wait()
        later[(slot - 1) * ROWS : slot * ROWS, :] = held[slot]
    start.wait()
    block = piece[...].astype(BF)
    wide = jnp.concatenate([block[q * 32 : q * 32 + 32] for q in range(4)], axis=1)
    fetch(low_inv, 0, 0).wait()
    for to in range(FRONT):
        send[to, 0:32, :] = wide
        send[to, 32:64, :] = held[0]


def spread_kernel(block, targets, spread):
    places = leaf_places(targets[...])
    for part in range(3):
        hot = one_hot(part * SEP, SEP, places)
        spread[part * SEP : part * SEP + SEP, :] = dot(hot, block[0], NN).astype(BF)


def stage_kernel(targets, later, block, leaf_targets, hot2, hot3, staged, picked, sem):
    leaf = lax.axis_index("leaf")
    copy = pltpu.make_async_copy(later, staged, sem)
    copy.start()
    hot2[...] = one_hot(0, SEP, targets[pl.ds(leaf >> 3, 1), :])
    hot3[...] = one_hot(0, 2 * SEP, ancestor_places(targets[pl.ds(2 + (leaf >> 2), 1), :]))
    places = leaf_places(leaf_targets[...])
    for part in range(3):
        hot = one_hot(part * SEP, SEP, places)
        picked[:, part * SEP : part * SEP + SEP] = dot(block[0], hot, NT).astype(BF)
    copy.wait()


def leaf_forward_kernel(got, inverse, spread, top, solved_out, send, mat, source):
    leaf = lax.axis_index("leaf")
    front = lax.axis_index("front")
    mat[...] = got[:, 32:64, :].reshape(SEP, SEP)
    for k in range(FRONT):
        for q in range(4):
            source[k * PIECE + q * 32 : k * PIECE + q * 32 + 32, :] = got[k, 0:32, q * RHS : q * RHS + RHS]
    solved = dot(inverse[0], source[...], NN)
    solved_out[...] = solved
    own = jnp.concatenate(
        [
            top[0] * (1 / 16),
            top[1 + (leaf >> 3)] * (1 / 8),
            top[3 + (leaf >> 2)] * (1 / 4),
            jnp.zeros((32, RHS), F32),
        ],
        axis=0,
    ).T
    row = lax.broadcasted_iota(jnp.int32, (RHS, SPAN), 0)
    column = lax.broadcasted_iota(jnp.int32, (RHS, SPAN), 1)
    hot = jnp.where(column == ((row >> 5) << 9) + front * ROWS + (row & 31), 1.0, 0.0).astype(BF)
    total = dot(own.astype(BF), hot, NN) - dot(solved.T.astype(BF), spread[...], NT)
    for to in range(FRONT):
        send[to] = fold(total[to * 8 : to * 8 + 8]).astype(BF)


def top_forward_kernel(got, first, beside, across, corner, targets, send, mats):
    leaf = lax.axis_index("leaf")
    role = leaf & 3
    mats[role] = first[...]
    mats[role ^ 1] = beside[...]
    mats[role ^ 2] = across[...]
    mats[role ^ 3] = corner[...]
    total = got[0].astype(F32)
    for k in range(1, FRONT):
        total = total + got[k].astype(F32)
    total = unfold(total)
    target1 = total[:, :SEP]
    target2 = total[:, SEP : 2 * SEP]
    target3 = total[:, 2 * SEP :]
    solved3 = split_dot(target3, mats[0], NT)
    update3 = split_dot(solved3, mats[1], NN)
    places3 = ancestor_places(targets[pl.ds(2 + (leaf >> 2), 1), :])
    spread3 = split_dot(update3, one_hot(0, 2 * SEP, places3), NT)
    target1 = target1 - spread3[:, :SEP]
    target2 = target2 - spread3[:, SEP:]
    solved2 = split_dot(target2, mats[2], NT)
    update2 = split_dot(solved2, mats[3], NN)
    places2 = targets[pl.ds(leaf >> 3, 1), :]
    target1 = target1 - split_dot(update2, one_hot(0, SEP, places2), NT)
    send[...] = fold(jnp.concatenate([target1, solved2, solved3], axis=1)).astype(BF)


def group_kernel(own, a, b, c, send):
    total = (own[...].astype(F32) + a[...].astype(F32)) + (b[...].astype(F32) + c[...].astype(F32))
    send[...] = total.astype(BF)


def top_backward_kernel(own, near, far, other, later, swapped, hot2, hot3, send):
    core = lax.axis_index("leaf") & 1
    part = unfold(own[...].astype(F32))
    side = unfold(near[...].astype(F32))
    rest = unfold(far[...].astype(F32) + other[...].astype(F32))
    total1 = part[:, :SEP] + side[:, :SEP] + rest[:, :SEP]
    total2 = part[:, SEP : 2 * SEP] + side[:, SEP : 2 * SEP]
    total3 = part[:, 2 * SEP :]

    def run(first, last):
        mats = [ref[:, i * ROWS : i * ROWS + ROWS, :].reshape(SEP, SEP) for ref in (first, last) for i in range(3)]
        x1 = split_dot(split_dot(total1, mats[0], NT), mats[1], NT)
        picked2 = split_dot(x1, hot2[...], NN)
        x2 = split_dot(total2 - split_dot(picked2, mats[2], NT), mats[3], NT)
        picked3 = split_dot(jnp.concatenate([x1, x2], axis=1), hot3[...], NN)
        x3 = split_dot(total3 - split_dot(picked3, mats[4], NT), mats[5], NT)
        out = fold(jnp.concatenate([x1, x2, x3], axis=1)).astype(BF)
        for to in range(FRONT):
            send[to] = out

    @pl.when(core == 0)
    def _():
        run(later, swapped)

    @pl.when(core == 1)
    def _():
        run(swapped, later)


def leaf_backward_kernel(got, solved, picked, send, own, side):
    front = lax.axis_index("front")
    full = jnp.concatenate([unfold(got[k].astype(F32)) for k in range(FRONT)], axis=0).astype(BF)
    residue = (solved[...] - dot(picked[...], full, NT)).astype(BF)
    for to in range(FRONT):
        send[to] = residue
    row = lax.broadcasted_iota(jnp.int32, (96, SPAN), 0)
    column = lax.broadcasted_iota(jnp.int32, (96, SPAN), 1)
    pick = jnp.where(column == ((row >> 5) << 9) + front * ROWS + (row & 31), 1.0, 0.0).astype(BF)
    rows = dot(pick, full, NT)
    own[...] = rows
    side[...] = rows[32:96, :].astype(BF)


def finish_kernel(got, inverse, own, near, far, other, leaf_out, top_out):
    leaf = lax.axis_index("leaf")
    leaf_out[0] = dot(inverse[0], got[...].reshape(SUB, RHS), NN)
    second = leaf >> 3
    third = leaf >> 2
    top_out[0] = own[0:32, :]
    top_out[1 + second] = own[32:64, :]
    top_out[1 + (second ^ 1)] = far[0:32, :].astype(F32)
    top_out[3 + third] = own[64:96, :]
    top_out[3 + (third ^ 1)] = near[32:64, :].astype(F32)
    top_out[3 + (third ^ 2)] = far[32:64, :].astype(F32)
    top_out[3 + (third ^ 3)] = other[32:64, :].astype(F32)


VMEM = pl.BlockSpec(memory_space=pltpu.VMEM)
HBM = pl.BlockSpec(memory_space=pltpu.HBM)


def keep(x):
    return pltpu.with_memory_space_constraint(x, pltpu.HBM)


def call(kernel, outs, args, specs=None, scratch=(), flops=0, size=0):
    shapes = [jax.ShapeDtypeStruct(shape, kind) for shape, kind in outs]
    return pl.pallas_call(
        kernel,
        out_shape=shapes,
        in_specs=specs or [VMEM] * len(args),
        out_specs=[VMEM] * len(shapes),
        scratch_shapes=list(scratch),
        compiler_params=pltpu.CompilerParams(vmem_limit_bytes=32 * 1024 * 1024),
        cost_estimate=pl.CostEstimate(flops=flops, bytes_accessed=size, transcendentals=0),
    )(*args)


def swap(x, flip):
    return lax.ppermute(x, "leaf", [(i, i ^ flip) for i in range(LEAVES)])


def exchange(x, axis, groups=None):
    return lax.all_to_all(x, axis, 0, 0, tiled=True, axis_index_groups=groups)


def body(
    leaf_source,
    top_source,
    leaf_lower_inverse,
    leaf_upper_inverse,
    leaf_lower_block,
    leaf_upper_block,
    top_lower_inverse,
    top_upper_inverse,
    top_lower_block,
    top_upper_block,
    leaf_targets,
    top_targets,
):
    send, later = call(
        prepare_kernel,
        [((FRONT, 64, SEP), BF), ((96, SEP), BF)],
        (
            keep(leaf_source),
            keep(top_lower_inverse),
            keep(top_upper_inverse),
            keep(jnp.swapaxes(top_lower_block, 1, 2)),
            keep(top_upper_block),
        ),
        specs=[HBM] * 5,
        scratch=[
            pltpu.VMEM((PIECE, RHS), F32),
            pltpu.VMEM((4, ROWS, SEP), BF),
            pltpu.SemaphoreType.DMA((5,)),
        ],
        size=3 << 20,
    )
    later = lax.all_gather(later, "front", axis=0, tiled=False)
    send, leaf_lower_block = lax.optimization_barrier((send, leaf_lower_block))
    got = exchange(send, "front")
    (spread,) = call(
        spread_kernel,
        [((SPAN, PIECE), BF)],
        (leaf_lower_block, leaf_targets),
        flops=2 * UPD * SPAN * PIECE,
        size=2 << 20,
    )
    solved, send, first = call(
        leaf_forward_kernel,
        [((PIECE, RHS), F32), ((FRONT, 16, HALF), BF), ((SEP, SEP), BF)],
        (got, leaf_lower_inverse, spread, top_source),
        scratch=[pltpu.VMEM((SUB, RHS), BF)],
        flops=2 * RHS * (PIECE * SUB + PIECE * SPAN),
        size=4 << 20,
    )
    across = swap(first, 2)
    beside = swap(first, 1)
    got = exchange(send, "front")
    across, got = lax.optimization_barrier((across, got))
    corner = swap(across, 1)
    (send,) = call(
        top_forward_kernel,
        [((16, HALF), BF)],
        (got, first, beside, across, corner, top_targets),
        scratch=[pltpu.VMEM((4, SEP, SEP), BF)],
        flops=2 * 256 * SEP * SEP * 8,
        size=4 << 20,
    )
    (total,) = call(
        group_kernel, [((16, HALF), BF)], (send, swap(send, 1), swap(send, 2), swap(send, 3)), size=1 << 17
    )
    near, far, other = swap(total, 4), swap(total, 8), swap(total, 12)
    later, near, far, other = lax.optimization_barrier((later, near, far, other))
    hot2, hot3, staged, picked = call(
        stage_kernel,
        [((SEP, SEP), BF), ((2 * SEP, SEP), BF), ((FRONT, 96, SEP), BF), ((PIECE, SPAN), BF)],
        (top_targets, keep(later), leaf_upper_block, leaf_targets),
        specs=[VMEM, HBM, VMEM, VMEM],
        scratch=[pltpu.SemaphoreType.DMA],
        flops=2 * UPD * SPAN * PIECE,
        size=2 << 20,
    )
    (send,) = call(
        top_backward_kernel,
        [((FRONT, 16, HALF), BF)],
        (total, near, far, other, staged, swap(later, 1), hot2, hot3),
        flops=2 * 256 * SEP * SEP * 9,
        size=5 << 20,
    )
    got = exchange(send, "front")
    send, own, side = call(
        leaf_backward_kernel,
        [((FRONT, PIECE, RHS), BF), ((96, RHS), F32), ((64, RHS), BF)],
        (got, solved, picked),
        flops=2 * RHS * 2 * PIECE * SPAN,
        size=2 << 20,
    )
    near, far, other = swap(side, 4), swap(side, 8), swap(side, 12)
    got = exchange(send, "front")
    leaf_solution, top_solution = call(
        finish_kernel,
        [((1, PIECE, RHS), F32), ((7, ROWS, RHS), F32)],
        (got, leaf_upper_inverse, own, near, far, other),
        flops=2 * RHS * PIECE * SUB,
        size=2 << 20,
    )
    return leaf_solution, top_solution


def solution(mesh):
    in_specs = (
        P("leaf", "front", None),
        P(None, "front", None),
        P("leaf", "front", None),
        P("leaf", "front", None),
        P("leaf", None, "front"),
        P("leaf", "front", None),
        P(None, "front", None),
        P(None, "front", None),
        P(None, None, "front"),
        P(None, "front", None),
        P("leaf", None),
        P(),
    )
    out_specs = (P("leaf", "front", None), P(None, "front", None))
    return jax.shard_map(body, mesh=mesh, in_specs=in_specs, out_specs=out_specs, check_vma=False)
```

```python
import jax
import jax.numpy as jnp
from jax import lax
from jax.experimental import pallas as pl
from jax.experimental.pallas import tpu as pltpu
from jax.sharding import PartitionSpec as P

BF = jnp.bfloat16
F32 = jnp.float32
FRONT = 16
LEAVES = 16
SUB = 2048
SEP = 512
UPD = 1024
RHS = 128
ROWS = SEP // FRONT
SPAN = 3 * SEP
HALF = SPAN // 2
PIECE = SUB // FRONT
NT = (((1,), (1,)), ((), ()))
NN = (((1,), (0,)), ((), ()))


def dot(a, b, dims):
    return lax.dot_general(a, b, dims, preferred_element_type=F32)


def split_dot(x, w, dims):
    head = x.astype(BF).astype(F32)
    both = jnp.concatenate([head, x - head], axis=0).astype(BF)
    out = dot(both, w, dims)
    return out[:8] + out[8:]


def fold(x):
    return jnp.concatenate([x[:, :HALF], x[:, HALF:]], axis=0)


def unfold(x):
    return jnp.concatenate([x[:8], x[8:]], axis=1)


def one_hot(first, count, places):
    rows = lax.broadcasted_iota(jnp.int32, (count, places.shape[1]), 0) + first
    return jnp.where(rows == places, 1.0, 0.0).astype(BF)


def leaf_places(targets):
    owner = targets >> 9
    height = jnp.where(owner > 0, 1, 0) + jnp.where(owner > 2, 1, 0)
    return (height << 9) | (targets & (SEP - 1))


def ancestor_places(targets):
    return jnp.where(targets >= SEP, SEP, 0) + (targets & (SEP - 1))


def prepare_kernel(source, low_inv, up_inv, low, up, send, piece, held, sems):
    leaf = lax.axis_index("leaf")
    third = 3 + (leaf >> 2)
    second = 1 + (leaf >> 3)
    role = leaf & 3
    whole, upper, lower = pl.ds(0, 32), pl.ds(0, 16), pl.ds(16, 16)
    even = [(low_inv, third, whole), (low_inv, second, whole)]
    odd = [(low, third - 1, whole), (low, second - 1, whole)]
    plans = [
        even + [(low_inv, 0, whole), (up_inv, 0, upper)],
        odd + [(up_inv, 0, lower), (up, second - 1, whole)],
        even + [(up_inv, second, whole), (up, third - 1, upper)],
        odd + [(up, third - 1, lower), (up_inv, third, whole)],
    ]
    start = pltpu.make_async_copy(source.at[0], piece, sems.at[4])
    start.start()
    for r, plan in enumerate(plans):

        @pl.when(role == r)
        def _(plan=plan):
            first = 0
            copies = []
            for slot, (ref, index, rows) in enumerate(plan):
                place = held.at[pl.ds(first, rows.size)]
                copies.append(pltpu.make_async_copy(ref.at[index, rows], place, sems.at[slot]))
                first += rows.size
            for copy in copies:
                copy.start()
            for copy in copies:
                copy.wait()

    start.wait()
    block = piece[...].astype(BF)
    wide = jnp.concatenate([block[q * 32 : q * 32 + 32] for q in range(4)], axis=1)
    mats = held[...]
    for to in range(FRONT):
        send[to, 0:32, :] = wide
        send[to, 32:144, :] = mats


def pick_kernel(block, targets, picked):
    places = leaf_places(targets[...])
    for part in range(3):
        rows = slice(part * SEP, part * SEP + SEP)
        picked[:, rows] = dot(block[0], one_hot(part * SEP, SEP, places), NT).astype(BF)


def leaf_forward_kernel(got, inverse, block, targets, top, solved_out, send, later, source):
    leaf = lax.axis_index("leaf")
    front = lax.axis_index("front")
    later[...] = got[:, 96:144, :]
    for k in range(FRONT):
        for q in range(4):
            source[k * PIECE + q * 32 : k * PIECE + q * 32 + 32, :] = got[k, 0:32, q * RHS : q * RHS + RHS]
    solved = dot(inverse[0], source[...], NN)
    solved_out[...] = solved
    update = dot(solved.T.astype(BF), block[0], NT)
    own = jnp.concatenate(
        [
            top[0] * (1 / 16),
            top[1 + (leaf >> 3)] * (1 / 8),
            top[3 + (leaf >> 2)] * (1 / 4),
            jnp.zeros((32, RHS), F32),
        ],
        axis=0,
    ).T
    lhs = jnp.concatenate([-update, own], axis=1).astype(BF)
    lane = lax.broadcasted_iota(jnp.int32, (1, RHS), 1)
    top_places = jnp.where(lane < 96, ((lane >> 5) << 9) + front * ROWS + (lane & 31), -1)
    places = jnp.concatenate([leaf_places(targets[...]), top_places], axis=1)
    low = dot(lhs, one_hot(0, HALF, places), NT)
    high = dot(lhs, one_hot(HALF, HALF, places), NT)
    for to in range(FRONT):
        rows = slice(to * 8, to * 8 + 8)
        send[to] = jnp.concatenate([low[rows], high[rows]], axis=0).astype(BF)


def by_role(refs, run):
    role = lax.axis_index("leaf") & 3
    for r in range(4):

        @pl.when(role == r)
        def _(r=r):
            run([refs[k ^ r] for k in range(4)])


def top_forward_kernel(got, first, swapped, targets, send, hot2, hot3):
    leaf = lax.axis_index("leaf")
    hot2[...] = one_hot(0, SEP, targets[pl.ds(leaf >> 3, 1), :])
    hot3[...] = one_hot(0, 2 * SEP, ancestor_places(targets[pl.ds(2 + (leaf >> 2), 1), :]))
    total = got[0].astype(F32)
    for k in range(1, FRONT):
        total = total + got[k].astype(F32)
    total = unfold(total)

    def run(*refs):
        even, odd = [[ref[:, i : i + 32, :].reshape(SEP, SEP) for i in (32, 64)] for ref in refs]
        target1 = total[:, :SEP]
        target2 = total[:, SEP : 2 * SEP]
        solved3 = split_dot(total[:, 2 * SEP :], even[0], NT)
        update3 = split_dot(solved3, odd[0], NN)
        spread3 = split_dot(update3, hot3[...], NT)
        target1 = target1 - spread3[:, :SEP]
        target2 = target2 - spread3[:, SEP:]
        solved2 = split_dot(target2, even[1], NT)
        update2 = split_dot(solved2, odd[1], NN)
        target1 = target1 - split_dot(update2, hot2[...], NT)
        send[...] = fold(jnp.concatenate([target1, solved2, solved3], axis=1)).astype(BF)

    @pl.when((leaf & 1) == 0)
    def _():
        run(first, swapped)

    @pl.when((leaf & 1) == 1)
    def _():
        run(swapped, first)


def group_kernel(own, a, b, c, send):
    total = (own[...].astype(F32) + a[...].astype(F32)) + (b[...].astype(F32) + c[...].astype(F32))
    send[...] = total.astype(BF)


def top_backward_kernel(own, near, far, other, first, beside, across, corner, hot2, hot3, send):
    part = unfold(own[...].astype(F32))
    side = unfold(near[...].astype(F32))
    rest = unfold(far[...].astype(F32) + other[...].astype(F32))
    total1 = part[:, :SEP] + side[:, :SEP] + rest[:, :SEP]
    total2 = part[:, SEP : 2 * SEP] + side[:, SEP : 2 * SEP]
    total3 = part[:, 2 * SEP :]

    def run(refs):
        mats = []
        for a, b in ((refs[0], refs[1]), (refs[2], refs[3])):
            i, j = a.shape[1] - 48, b.shape[1] - 48
            mats.append(a[:, i : i + 32, :].reshape(SEP, SEP))
            mats.append(jnp.concatenate([a[:, i + 32 : i + 48, :], b[:, j : j + 16, :]], axis=1).reshape(SEP, SEP))
            mats.append(b[:, j + 16 : j + 48, :].reshape(SEP, SEP))
        x1 = split_dot(split_dot(total1, mats[0], NT), mats[1], NT)
        picked2 = split_dot(x1, hot2[...], NN)
        x2 = split_dot(total2 - split_dot(picked2, mats[2], NT), mats[3], NT)
        picked3 = split_dot(jnp.concatenate([x1, x2], axis=1), hot3[...], NN)
        x3 = split_dot(total3 - split_dot(picked3, mats[4], NT), mats[5], NT)
        out = fold(jnp.concatenate([x1, x2, x3], axis=1)).astype(BF)
        for to in range(FRONT):
            send[to] = out

    by_role([first, beside, across, corner], run)


def leaf_backward_kernel(got, solved, picked, send, own, side):
    front = lax.axis_index("front")
    full = jnp.concatenate([unfold(got[k].astype(F32)) for k in range(FRONT)], axis=0).astype(BF)
    residue = (solved[...] - dot(picked[...], full, NT)).astype(BF)
    for to in range(FRONT):
        send[to] = residue
    row = lax.broadcasted_iota(jnp.int32, (96, SPAN), 0)
    column = lax.broadcasted_iota(jnp.int32, (96, SPAN), 1)
    pick = jnp.where(column == ((row >> 5) << 9) + front * ROWS + (row & 31), 1.0, 0.0).astype(BF)
    rows = dot(pick, full, NT)
    own[...] = rows
    side[...] = rows[32:96, :].astype(BF)


def finish_kernel(got, inverse, own, near, far, other, leaf_out, top_out):
    leaf = lax.axis_index("leaf")
    leaf_out[0] = dot(inverse[0], got[...].reshape(SUB, RHS), NN)
    second = leaf >> 3
    third = leaf >> 2
    top_out[0] = own[0:32, :]
    top_out[1 + second] = own[32:64, :]
    top_out[1 + (second ^ 1)] = far[0:32, :].astype(F32)
    top_out[3 + third] = own[64:96, :]
    top_out[3 + (third ^ 1)] = near[32:64, :].astype(F32)
    top_out[3 + (third ^ 2)] = far[32:64, :].astype(F32)
    top_out[3 + (third ^ 3)] = other[32:64, :].astype(F32)


VMEM = pl.BlockSpec(memory_space=pltpu.VMEM)
HBM = pl.BlockSpec(memory_space=pltpu.HBM)


def keep(x):
    return pltpu.with_memory_space_constraint(x, pltpu.HBM)


def call(kernel, outs, args, specs=None, scratch=(), flops=0, size=0):
    shapes = [jax.ShapeDtypeStruct(shape, kind) for shape, kind in outs]
    return pl.pallas_call(
        kernel,
        out_shape=shapes,
        in_specs=specs or [VMEM] * len(args),
        out_specs=[VMEM] * len(shapes),
        scratch_shapes=list(scratch),
        compiler_params=pltpu.CompilerParams(vmem_limit_bytes=16 * 1024 * 1024),
        cost_estimate=pl.CostEstimate(flops=flops, bytes_accessed=size, transcendentals=0),
    )(*args)


def swap(x, flip):
    return lax.ppermute(x, "leaf", [(i, i ^ flip) for i in range(LEAVES)])


def exchange(x, axis, groups=None):
    return lax.all_to_all(x, axis, 0, 0, tiled=True, axis_index_groups=groups)


def body(
    leaf_source,
    top_source,
    leaf_lower_inverse,
    leaf_upper_inverse,
    leaf_lower_block,
    leaf_upper_block,
    top_lower_inverse,
    top_upper_inverse,
    top_lower_block,
    top_upper_block,
    leaf_targets,
    top_targets,
):
    (send,) = call(
        prepare_kernel,
        [((FRONT, 144, SEP), BF)],
        (
            keep(leaf_source),
            keep(top_lower_inverse),
            keep(top_upper_inverse),
            keep(jnp.swapaxes(top_lower_block, 1, 2)),
            keep(top_upper_block),
        ),
        specs=[HBM] * 5,
        scratch=[
            pltpu.VMEM((PIECE, RHS), F32),
            pltpu.VMEM((112, SEP), BF),
            pltpu.SemaphoreType.DMA((5,)),
        ],
        size=3 << 20,
    )
    got = exchange(send, "front")
    swapped = swap(got, 1)
    first = got
    solved, send, later = call(
        leaf_forward_kernel,
        [((PIECE, RHS), F32), ((FRONT, 16, HALF), BF), ((FRONT, 48, SEP), BF)],
        (got, leaf_lower_inverse, leaf_lower_block, leaf_targets, top_source),
        scratch=[pltpu.VMEM((SUB, RHS), BF)],
        flops=2 * RHS * (PIECE * SUB + UPD * PIECE + UPD * SPAN),
        size=4 << 20,
    )
    across = swap(later, 2)
    got = exchange(send, "front")
    send, hot2, hot3 = call(
        top_forward_kernel,
        [((16, HALF), BF), ((SEP, SEP), BF), ((2 * SEP, SEP), BF)],
        (got, first, swapped, top_targets),
        flops=2 * 256 * SEP * SEP * 8,
        size=4 << 20,
    )
    (total,) = call(
        group_kernel, [((16, HALF), BF)], (send, swap(send, 1), swap(send, 2), swap(send, 3)), size=1 << 17
    )
    near, far, other = swap(total, 4), swap(total, 8), swap(total, 12)
    across, total, leaf_upper_block = lax.optimization_barrier((across, total, leaf_upper_block))
    (picked,) = call(
        pick_kernel,
        [((PIECE, SPAN), BF)],
        (leaf_upper_block, leaf_targets),
        flops=2 * UPD * SPAN * PIECE,
        size=2 << 20,
    )
    near, picked = lax.optimization_barrier((near, picked))
    (send,) = call(
        top_backward_kernel,
        [((FRONT, 16, HALF), BF)],
        (total, near, far, other, first, swapped, across, swap(across, 1), hot2, hot3),
        flops=2 * 256 * SEP * SEP * 9,
        size=5 << 20,
    )
    got = exchange(send, "front")
    send, own, side = call(
        leaf_backward_kernel,
        [((FRONT, PIECE, RHS), BF), ((96, RHS), F32), ((64, RHS), BF)],
        (got, solved, picked),
        flops=2 * RHS * 2 * PIECE * SPAN,
        size=2 << 20,
    )
    near, far, other = swap(side, 4), swap(side, 8), swap(side, 12)
    got = exchange(send, "front")
    leaf_solution, top_solution = call(
        finish_kernel,
        [((1, PIECE, RHS), F32), ((7, ROWS, RHS), F32)],
        (got, leaf_upper_inverse, own, near, far, other),
        flops=2 * RHS * PIECE * SUB,
        size=2 << 20,
    )
    return leaf_solution, top_solution


def solution(mesh):
    in_specs = (
        P("leaf", "front", None),
        P(None, "front", None),
        P("leaf", "front", None),
        P("leaf", "front", None),
        P("leaf", None, "front"),
        P("leaf", "front", None),
        P(None, "front", None),
        P(None, "front", None),
        P(None, None, "front"),
        P(None, "front", None),
        P("leaf", None),
        P(),
    )
    out_specs = (P("leaf", "front", None), P(None, "front", None))
    return jax.shard_map(body, mesh=mesh, in_specs=in_specs, out_specs=out_specs, check_vma=False)
```

```python
import jax
import jax.numpy as jnp
from jax import lax
from jax.experimental import pallas as pl
from jax.experimental.pallas import tpu as pltpu
from jax.sharding import PartitionSpec as P

BF = jnp.bfloat16
F32 = jnp.float32
FRONT = 16
LEAVES = 16
SUB = 2048
SEP = 512
UPD = 1024
RHS = 128
ROWS = SEP // FRONT
SPAN = 3 * SEP
HALF = SPAN // 2
PIECE = SUB // FRONT
NT = (((1,), (1,)), ((), ()))
NN = (((1,), (0,)), ((), ()))


def dot(a, b, dims):
    return lax.dot_general(a, b, dims, preferred_element_type=F32)


def split_dot(x, w, dims):
    head = x.astype(BF).astype(F32)
    both = jnp.concatenate([head, x - head], axis=0).astype(BF)
    out = dot(both, w, dims)
    return out[:8] + out[8:]


def fold(x):
    return jnp.concatenate([x[:, :HALF], x[:, HALF:]], axis=0)


def unfold(x):
    return jnp.concatenate([x[:8], x[8:]], axis=1)


def one_hot(first, count, places):
    rows = lax.broadcasted_iota(jnp.int32, (count, places.shape[1]), 0) + first
    return jnp.where(rows == places, 1.0, 0.0).astype(BF)


def leaf_places(targets):
    owner = targets >> 9
    height = jnp.where(owner > 0, 1, 0) + jnp.where(owner > 2, 1, 0)
    return (height << 9) | (targets & (SEP - 1))


def ancestor_places(targets):
    return jnp.where(targets >= SEP, SEP, 0) + (targets & (SEP - 1))


def prepare_kernel(source, low_inv, up_inv, low, up, send, mats, piece, sems):
    leaf = lax.axis_index("leaf")
    third = 3 + (leaf >> 2)
    second = 1 + (leaf >> 3)
    plans = [
        [(low_inv, third), (low_inv, second), (low_inv, 0), (up_inv, 0), (up, second - 1)],
        [(low, third - 1), (low, second - 1), (up_inv, second), (up, third - 1), (up_inv, third)],
    ]
    places = [mats.at[pl.ds(i * ROWS, ROWS)] for i in range(5)]
    start = pltpu.make_async_copy(source.at[0], piece, sems.at[5])
    start.start()
    for core, plan in enumerate(plans):

        @pl.when((leaf & 1) == core)
        def _(plan=plan):
            copies = [
                pltpu.make_async_copy(ref.at[index], place, sems.at[slot])
                for slot, ((ref, index), place) in enumerate(zip(plan, places))
            ]
            for copy in copies:
                copy.start()
            for copy in copies:
                copy.wait()

    start.wait()
    block = piece[...].astype(BF)
    for to in range(FRONT):
        send[to] = block


def pack_kernel(own, a, b, c, out):
    for k, ref in enumerate((own, a, b, c)):
        out[k] = ref[...]


def assemble_kernel(own, a, b, c, ahead, later):
    front = lax.axis_index("front")
    core = lax.axis_index("leaf") & 1
    y, x = front >> 2, front & 3
    for j, ref in enumerate((own, a, b, c)):
        for k in range(4):
            dy = jnp.where(core == 0, j, k)
            dx = jnp.where(core == 0, k, j)
            at = ((y - dy) & 3) * 4 + ((x - dx) & 3)
            rows = pl.ds(pl.multiple_of(at * ROWS, ROWS), ROWS)
            for i in range(5):
                part = ref[k, i * ROWS : i * ROWS + ROWS, :]
                if i < 2:
                    ahead[i, rows, :] = part
                else:
                    later[i - 2, rows, :] = part


def pick_kernel(block, targets, picked):
    places = leaf_places(targets[...])
    for part in range(3):
        rows = slice(part * SEP, part * SEP + SEP)
        picked[:, rows] = dot(block[0], one_hot(part * SEP, SEP, places), NT).astype(BF)


def leaf_forward_kernel(got, inverse, block, targets, top, solved_out, send):
    leaf = lax.axis_index("leaf")
    front = lax.axis_index("front")
    solved = dot(inverse[0], got[...].reshape(SUB, RHS), NN)
    solved_out[...] = solved
    update = dot(solved.T.astype(BF), block[0], NT)
    own = jnp.concatenate(
        [
            top[0] * (1 / 16),
            top[1 + (leaf >> 3)] * (1 / 8),
            top[3 + (leaf >> 2)] * (1 / 4),
            jnp.zeros((32, RHS), F32),
        ],
        axis=0,
    ).T
    lhs = jnp.concatenate([-update, own], axis=1).astype(BF)
    lane = lax.broadcasted_iota(jnp.int32, (1, RHS), 1)
    top_places = jnp.where(lane < 96, ((lane >> 5) << 9) + front * ROWS + (lane & 31), -1)
    places = jnp.concatenate([leaf_places(targets[...]), top_places], axis=1)
    low = dot(lhs, one_hot(0, HALF, places), NT)
    high = dot(lhs, one_hot(HALF, HALF, places), NT)
    for to in range(FRONT):
        rows = slice(to * 8, to * 8 + 8)
        send[to] = jnp.concatenate([low[rows], high[rows]], axis=0).astype(BF)


def top_forward_kernel(got, first, swapped, targets, send, hot2, hot3):
    leaf = lax.axis_index("leaf")
    hot2[...] = one_hot(0, SEP, targets[pl.ds(leaf >> 3, 1), :])
    hot3[...] = one_hot(0, 2 * SEP, ancestor_places(targets[pl.ds(2 + (leaf >> 2), 1), :]))
    total = got[0].astype(F32)
    for k in range(1, FRONT):
        total = total + got[k].astype(F32)
    total = unfold(total)

    def run(even, odd):
        target1 = total[:, :SEP]
        target2 = total[:, SEP : 2 * SEP]
        solved3 = split_dot(total[:, 2 * SEP :], even[0], NT)
        update3 = split_dot(solved3, odd[0], NN)
        spread3 = split_dot(update3, hot3[...], NT)
        target1 = target1 - spread3[:, :SEP]
        target2 = target2 - spread3[:, SEP:]
        solved2 = split_dot(target2, even[1], NT)
        update2 = split_dot(solved2, odd[1], NN)
        target1 = target1 - split_dot(update2, hot2[...], NT)
        send[...] = fold(jnp.concatenate([target1, solved2, solved3], axis=1)).astype(BF)

    @pl.when((leaf & 1) == 0)
    def _():
        run(first, swapped)

    @pl.when((leaf & 1) == 1)
    def _():
        run(swapped, first)


def group_kernel(own, a, b, c, send):
    total = (own[...].astype(F32) + a[...].astype(F32)) + (b[...].astype(F32) + c[...].astype(F32))
    send[...] = total.astype(BF)


def top_backward_kernel(own, near, far, other, later, swapped, hot2, hot3, send):
    core = lax.axis_index("leaf") & 1
    part = unfold(own[...].astype(F32))
    side = unfold(near[...].astype(F32))
    rest = unfold(far[...].astype(F32) + other[...].astype(F32))
    total1 = part[:, :SEP] + side[:, :SEP] + rest[:, :SEP]
    total2 = part[:, SEP : 2 * SEP] + side[:, SEP : 2 * SEP]
    total3 = part[:, 2 * SEP :]

    def run(first, last):
        mats = [first[0], first[1], first[2], last[0], last[1], last[2]]
        x1 = split_dot(split_dot(total1, mats[0], NT), mats[1], NT)
        picked2 = split_dot(x1, hot2[...], NN)
        x2 = split_dot(total2 - split_dot(picked2, mats[2], NT), mats[3], NT)
        picked3 = split_dot(jnp.concatenate([x1, x2], axis=1), hot3[...], NN)
        x3 = split_dot(total3 - split_dot(picked3, mats[4], NT), mats[5], NT)
        out = fold(jnp.concatenate([x1, x2, x3], axis=1)).astype(BF)
        for to in range(FRONT):
            send[to] = out

    @pl.when(core == 0)
    def _():
        run(later, swapped)

    @pl.when(core == 1)
    def _():
        run(swapped, later)


def leaf_backward_kernel(got, solved, picked, send, own, side):
    front = lax.axis_index("front")
    full = jnp.concatenate([unfold(got[k].astype(F32)) for k in range(FRONT)], axis=0).astype(BF)
    residue = (solved[...] - dot(picked[...], full, NT)).astype(BF)
    for to in range(FRONT):
        send[to] = residue
    row = lax.broadcasted_iota(jnp.int32, (96, SPAN), 0)
    column = lax.broadcasted_iota(jnp.int32, (96, SPAN), 1)
    pick = jnp.where(column == ((row >> 5) << 9) + front * ROWS + (row & 31), 1.0, 0.0).astype(BF)
    rows = dot(pick, full, NT)
    own[...] = rows
    side[...] = rows[32:96, :].astype(BF)


def finish_kernel(got, inverse, own, near, far, other, leaf_out, top_out):
    leaf = lax.axis_index("leaf")
    leaf_out[0] = dot(inverse[0], got[...].reshape(SUB, RHS), NN)
    second = leaf >> 3
    third = leaf >> 2
    top_out[0] = own[0:32, :]
    top_out[1 + second] = own[32:64, :]
    top_out[1 + (second ^ 1)] = far[0:32, :].astype(F32)
    top_out[3 + third] = own[64:96, :]
    top_out[3 + (third ^ 1)] = near[32:64, :].astype(F32)
    top_out[3 + (third ^ 2)] = far[32:64, :].astype(F32)
    top_out[3 + (third ^ 3)] = other[32:64, :].astype(F32)


VMEM = pl.BlockSpec(memory_space=pltpu.VMEM)
HBM = pl.BlockSpec(memory_space=pltpu.HBM)


def keep(x):
    return pltpu.with_memory_space_constraint(x, pltpu.HBM)


def call(kernel, outs, args, specs=None, scratch=(), flops=0, size=0):
    shapes = [jax.ShapeDtypeStruct(shape, kind) for shape, kind in outs]
    return pl.pallas_call(
        kernel,
        out_shape=shapes,
        in_specs=specs or [VMEM] * len(args),
        out_specs=[VMEM] * len(shapes),
        scratch_shapes=list(scratch),
        compiler_params=pltpu.CompilerParams(vmem_limit_bytes=16 * 1024 * 1024),
        cost_estimate=pl.CostEstimate(flops=flops, bytes_accessed=size, transcendentals=0),
    )(*args)


def swap(x, flip):
    return lax.ppermute(x, "leaf", [(i, i ^ flip) for i in range(LEAVES)])


def shifts(x, turn):
    def moved(leaf, front, k):
        y, x = front // 4, front % 4
        if (leaf + turn) % 2 == 0:
            return leaf * FRONT + y * 4 + (x + k) % 4
        return leaf * FRONT + (y + k) % 4 * 4 + x

    everyone = [(leaf, front) for leaf in range(LEAVES) for front in range(FRONT)]
    return [
        lax.ppermute(x, ("leaf", "front"), [(leaf * FRONT + front, moved(leaf, front, k)) for leaf, front in everyone])
        for k in (1, 2, 3)
    ]


def exchange(x, axis, groups=None):
    return lax.all_to_all(x, axis, 0, 0, tiled=True, axis_index_groups=groups)


def body(
    leaf_source,
    top_source,
    leaf_lower_inverse,
    leaf_upper_inverse,
    leaf_lower_block,
    leaf_upper_block,
    top_lower_inverse,
    top_upper_inverse,
    top_lower_block,
    top_upper_block,
    leaf_targets,
    top_targets,
):
    send, mats = call(
        prepare_kernel,
        [((FRONT, PIECE, RHS), BF), ((160, SEP), BF)],
        (
            keep(leaf_source),
            keep(top_lower_inverse),
            keep(top_upper_inverse),
            keep(jnp.swapaxes(top_lower_block, 1, 2)),
            keep(top_upper_block),
        ),
        specs=[HBM] * 5,
        scratch=[pltpu.VMEM((PIECE, RHS), F32), pltpu.SemaphoreType.DMA((6,))],
        size=1 << 20,
    )
    got = exchange(send, "front")
    got, mats, *parts = lax.optimization_barrier((got, mats, *shifts(mats, 0)))
    (mats,) = call(pack_kernel, [((4, 160, SEP), BF)], (mats, *parts), size=1 << 20)
    solved, send = call(
        leaf_forward_kernel,
        [((PIECE, RHS), F32), ((FRONT, 16, HALF), BF)],
        (got, leaf_lower_inverse, leaf_lower_block, leaf_targets, top_source),
        flops=2 * RHS * (PIECE * SUB + UPD * PIECE + UPD * SPAN),
        size=4 << 20,
    )
    parts = shifts(mats, 1)
    got = exchange(send, "front")
    got, *parts = lax.optimization_barrier((got, *parts))
    ahead, later = call(
        assemble_kernel, [((2, SEP, SEP), BF), ((3, SEP, SEP), BF)], (mats, *parts), size=5 << 20
    )
    send, hot2, hot3 = call(
        top_forward_kernel,
        [((16, HALF), BF), ((SEP, SEP), BF), ((2 * SEP, SEP), BF)],
        (got, ahead, swap(ahead, 1), top_targets),
        flops=2 * 256 * SEP * SEP * 8,
        size=4 << 20,
    )
    send, later = lax.optimization_barrier((send, later))
    (total,) = call(
        group_kernel, [((16, HALF), BF)], (send, swap(send, 1), swap(send, 2), swap(send, 3)), size=1 << 17
    )
    near, far, other = swap(total, 4), swap(total, 8), swap(total, 12)
    total, leaf_upper_block = lax.optimization_barrier((total, leaf_upper_block))
    (picked,) = call(
        pick_kernel,
        [((PIECE, SPAN), BF)],
        (leaf_upper_block, leaf_targets),
        flops=2 * UPD * SPAN * PIECE,
        size=2 << 20,
    )
    near, picked = lax.optimization_barrier((near, picked))
    (send,) = call(
        top_backward_kernel,
        [((FRONT, 16, HALF), BF)],
        (total, near, far, other, later, swap(later, 1), hot2, hot3),
        flops=2 * 256 * SEP * SEP * 9,
        size=5 << 20,
    )
    got = exchange(send, "front")
    send, own, side = call(
        leaf_backward_kernel,
        [((FRONT, PIECE, RHS), BF), ((96, RHS), F32), ((64, RHS), BF)],
        (got, solved, picked),
        flops=2 * RHS * 2 * PIECE * SPAN,
        size=2 << 20,
    )
    near, far, other = swap(side, 4), swap(side, 8), swap(side, 12)
    got = exchange(send, "front")
    leaf_solution, top_solution = call(
        finish_kernel,
        [((1, PIECE, RHS), F32), ((7, ROWS, RHS), F32)],
        (got, leaf_upper_inverse, own, near, far, other),
        flops=2 * RHS * PIECE * SUB,
        size=2 << 20,
    )
    return leaf_solution, top_solution


def solution(mesh):
    in_specs = (
        P("leaf", "front", None),
        P(None, "front", None),
        P("leaf", "front", None),
        P("leaf", "front", None),
        P("leaf", None, "front"),
        P("leaf", "front", None),
        P(None, "front", None),
        P(None, "front", None),
        P(None, None, "front"),
        P(None, "front", None),
        P("leaf", None),
        P(),
    )
    out_specs = (P("leaf", "front", None), P(None, "front", None))
    return jax.shard_map(body, mesh=mesh, in_specs=in_specs, out_specs=out_specs, check_vma=False)
```

```python
import jax
import jax.numpy as jnp
from jax import lax
from jax.experimental import pallas as pl
from jax.experimental.pallas import tpu as pltpu
from jax.sharding import PartitionSpec as P

BF = jnp.bfloat16
F32 = jnp.float32
FRONT = 16
LEAVES = 16
SUB = 2048
SEP = 512
UPD = 1024
RHS = 128
ROWS = SEP // FRONT
SPAN = 3 * SEP
HALF = SPAN // 2
PIECE = SUB // FRONT
NT = (((1,), (1,)), ((), ()))
NN = (((1,), (0,)), ((), ()))


def dot(a, b, dims):
    return lax.dot_general(a, b, dims, preferred_element_type=F32)


def split_dot(x, w, dims):
    head = x.astype(BF).astype(F32)
    both = jnp.concatenate([head, x - head], axis=0).astype(BF)
    out = dot(both, w, dims)
    return out[:8] + out[8:]


def fold(x):
    half = x.shape[1] // 2
    return jnp.concatenate([x[:, :half], x[:, half:]], axis=0)


def unfold(x):
    return jnp.concatenate([x[:8], x[8:]], axis=1)


def one_hot(first, count, places):
    rows = lax.broadcasted_iota(jnp.int32, (count, places.shape[1]), 0) + first
    return jnp.where(rows == places, 1.0, 0.0).astype(BF)


def leaf_places(targets):
    owner = targets >> 9
    height = jnp.where(owner > 0, 1, 0) + jnp.where(owner > 2, 1, 0)
    return (height << 9) | (targets & (SEP - 1))


def ancestor_places(targets):
    return jnp.where(targets >= SEP, SEP, 0) + (targets & (SEP - 1))


def prepare_kernel(source, low_inv, up_inv, low, up, send, mats, piece, sems):
    leaf = lax.axis_index("leaf")
    third = 3 + (leaf >> 2)
    second = 1 + (leaf >> 3)
    plans = [
        [(low_inv, third), (low_inv, second), (low_inv, 0), (up_inv, 0), (up, second - 1)],
        [(low, third - 1), (low, second - 1), (up_inv, second), (up, third - 1), (up_inv, third)],
    ]
    places = [mats.at[pl.ds(i * ROWS, ROWS)] for i in range(5)]
    start = pltpu.make_async_copy(source.at[0], piece, sems.at[5])
    start.start()
    for core, plan in enumerate(plans):

        @pl.when((leaf & 1) == core)
        def _(plan=plan):
            copies = [
                pltpu.make_async_copy(ref.at[index], place, sems.at[slot])
                for slot, ((ref, index), place) in enumerate(zip(plan, places))
            ]
            for copy in copies:
                copy.start()
            for copy in copies:
                copy.wait()

    start.wait()
    block = piece[...].astype(BF)
    for to in range(FRONT):
        send[to] = block


def pack_kernel(own, a, b, c, out):
    for k, ref in enumerate((own, a, b, c)):
        out[k] = ref[...]


def assemble_kernel(own, a, b, c, ahead, second, later):
    front = lax.axis_index("front")
    core = lax.axis_index("leaf") & 1
    y, x = front >> 2, front & 3
    for j, ref in enumerate((own, a, b, c)):
        for k in range(4):
            dy = jnp.where(core == 0, j, k)
            dx = jnp.where(core == 0, k, j)
            at = ((y - dy) & 3) * 4 + ((x - dx) & 3)
            rows = pl.ds(pl.multiple_of(at * ROWS, ROWS), ROWS)
            for i in range(5):
                part = ref[k, i * ROWS : i * ROWS + ROWS, :]
                if i < 2:
                    (ahead, second)[i][rows, :] = part
                else:
                    later[i - 2, rows, :] = part


def pick_kernel(block, targets, picked):
    places = leaf_places(targets[...])
    for part in range(3):
        rows = slice(part * SEP, part * SEP + SEP)
        picked[:, rows] = dot(block[0], one_hot(part * SEP, SEP, places), NT).astype(BF)


def spread_kernel(block, targets, spread):
    places = leaf_places(targets[...])
    for part in range(3):
        hot = one_hot(part * SEP, SEP, places)
        spread[part * SEP : part * SEP + SEP, :] = dot(hot, block[0], NN).astype(BF)


def leaf_forward_kernel(got, inverse, spread, top, solved_out, send):
    leaf = lax.axis_index("leaf")
    front = lax.axis_index("front")
    solved = dot(inverse[0], got[...].reshape(SUB, RHS), NN)
    solved_out[...] = solved
    own = jnp.concatenate(
        [
            top[0] * (1 / 16),
            top[1 + (leaf >> 3)] * (1 / 8),
            top[3 + (leaf >> 2)] * (1 / 4),
            jnp.zeros((32, RHS), F32),
        ],
        axis=0,
    ).T
    row = lax.broadcasted_iota(jnp.int32, (RHS, SPAN), 0)
    column = lax.broadcasted_iota(jnp.int32, (RHS, SPAN), 1)
    hot = jnp.where(column == ((row >> 5) << 9) + front * ROWS + (row & 31), 1.0, 0.0).astype(BF)
    total = dot(own.astype(BF), hot, NN) - dot(solved.T.astype(BF), spread[...], NT)
    for to in range(FRONT):
        send[to] = fold(total[to * 8 : to * 8 + 8]).astype(BF)


def top_forward_kernel(got, first, swapped, targets, send, hot2, hot3):
    leaf = lax.axis_index("leaf")
    hot2[...] = one_hot(0, SEP, targets[pl.ds(leaf >> 3, 1), :])
    hot3[...] = one_hot(0, 2 * SEP, ancestor_places(targets[pl.ds(2 + (leaf >> 2), 1), :]))
    total = got[0].astype(F32)
    for k in range(1, FRONT):
        total = total + got[k].astype(F32)
    total = unfold(total)

    def run(even, odd):
        solved3 = split_dot(total[:, 2 * SEP :], even[...], NT)
        update3 = split_dot(solved3, odd[...], NN)
        above = total[:, : 2 * SEP] - split_dot(update3, hot3[...], NT)
        send[...] = fold(jnp.concatenate([above, solved3], axis=1)).astype(BF)

    @pl.when((leaf & 1) == 0)
    def _():
        run(first, swapped)

    @pl.when((leaf & 1) == 1)
    def _():
        run(swapped, first)


def group_kernel(own, a, b, c, first, swapped, hot2, far, near, other):
    core = lax.axis_index("leaf") & 1
    total = (own[...].astype(F32) + a[...].astype(F32)) + (b[...].astype(F32) + c[...].astype(F32))
    total = unfold(total)

    def run(even, odd):
        solved2 = split_dot(total[:, SEP : 2 * SEP], even[...], NT)
        update2 = split_dot(solved2, odd[...], NN)
        target1 = total[:, :SEP] - split_dot(update2, hot2[...], NT)
        far[...] = fold(jnp.concatenate([target1, solved2, total[:, 2 * SEP :]], axis=1)).astype(BF)
        near[...] = fold(jnp.concatenate([target1, solved2], axis=1)).astype(BF)
        other[...] = fold(target1).astype(BF)

    @pl.when(core == 0)
    def _():
        run(first, swapped)

    @pl.when(core == 1)
    def _():
        run(swapped, first)


def top_backward_kernel(own, near, far, other, later, swapped, hot2, hot3, send):
    core = lax.axis_index("leaf") & 1
    part = unfold(own[...].astype(F32))
    side = unfold(near[...].astype(F32))
    total1 = part[:, :SEP] + side[:, :SEP] + unfold(far[...].astype(F32))[:, :SEP] + unfold(other[...].astype(F32))
    total2 = part[:, SEP : 2 * SEP] + side[:, SEP : 2 * SEP]
    total3 = part[:, 2 * SEP :]

    def run(first, last):
        mats = [first[0], first[1], first[2], last[0], last[1], last[2]]
        x1 = split_dot(split_dot(total1, mats[0], NT), mats[1], NT)
        picked2 = split_dot(x1, hot2[...], NN)
        x2 = split_dot(total2 - split_dot(picked2, mats[2], NT), mats[3], NT)
        picked3 = split_dot(jnp.concatenate([x1, x2], axis=1), hot3[...], NN)
        x3 = split_dot(total3 - split_dot(picked3, mats[4], NT), mats[5], NT)
        out = fold(jnp.concatenate([x1, x2, x3], axis=1)).astype(BF)
        for to in range(FRONT):
            send[to] = out

    @pl.when(core == 0)
    def _():
        run(later, swapped)

    @pl.when(core == 1)
    def _():
        run(swapped, later)


def leaf_backward_kernel(got, solved, picked, send, own, side, last):
    front = lax.axis_index("front")
    full = jnp.concatenate([unfold(got[k].astype(F32)) for k in range(FRONT)], axis=0).astype(BF)
    residue = (solved[...] - dot(picked[...], full, NT)).astype(BF)
    for to in range(FRONT):
        send[to] = residue
    row = lax.broadcasted_iota(jnp.int32, (96, SPAN), 0)
    column = lax.broadcasted_iota(jnp.int32, (96, SPAN), 1)
    pick = jnp.where(column == ((row >> 5) << 9) + front * ROWS + (row & 31), 1.0, 0.0).astype(BF)
    rows = dot(pick, full, NT)
    own[...] = rows
    side[...] = rows[32:96, :].astype(BF)
    last[...] = rows[64:96, :].astype(BF)


def finish_kernel(got, inverse, own, near, far, other, leaf_out, top_out):
    leaf = lax.axis_index("leaf")
    leaf_out[0] = dot(inverse[0], got[...].reshape(SUB, RHS), NN)
    second = leaf >> 3
    third = leaf >> 2
    top_out[0] = own[0:32, :]
    top_out[1 + second] = own[32:64, :]
    top_out[1 + (second ^ 1)] = far[0:32, :].astype(F32)
    top_out[3 + third] = own[64:96, :]
    top_out[3 + (third ^ 1)] = near[...].astype(F32)
    top_out[3 + (third ^ 2)] = far[32:64, :].astype(F32)
    top_out[3 + (third ^ 3)] = other[...].astype(F32)


VMEM = pl.BlockSpec(memory_space=pltpu.VMEM)
HBM = pl.BlockSpec(memory_space=pltpu.HBM)


def keep(x):
    return pltpu.with_memory_space_constraint(x, pltpu.HBM)


def call(kernel, outs, args, specs=None, scratch=(), flops=0, size=0):
    shapes = [jax.ShapeDtypeStruct(shape, kind) for shape, kind in outs]
    return pl.pallas_call(
        kernel,
        out_shape=shapes,
        in_specs=specs or [VMEM] * len(args),
        out_specs=[VMEM] * len(shapes),
        scratch_shapes=list(scratch),
        compiler_params=pltpu.CompilerParams(vmem_limit_bytes=16 * 1024 * 1024),
        cost_estimate=pl.CostEstimate(flops=flops, bytes_accessed=size, transcendentals=0),
    )(*args)


def swap(x, flip):
    return lax.ppermute(x, "leaf", [(i, i ^ flip) for i in range(LEAVES)])


def shifts(x, turn):
    def moved(leaf, front, k):
        y, x = front // 4, front % 4
        if (leaf + turn) % 2 == 0:
            return leaf * FRONT + y * 4 + (x + k) % 4
        return leaf * FRONT + (y + k) % 4 * 4 + x

    everyone = [(leaf, front) for leaf in range(LEAVES) for front in range(FRONT)]
    return [
        lax.ppermute(x, ("leaf", "front"), [(leaf * FRONT + front, moved(leaf, front, k)) for leaf, front in everyone])
        for k in (1, 2, 3)
    ]


def exchange(x, axis, groups=None):
    return lax.all_to_all(x, axis, 0, 0, tiled=True, axis_index_groups=groups)


def body(
    leaf_source,
    top_source,
    leaf_lower_inverse,
    leaf_upper_inverse,
    leaf_lower_block,
    leaf_upper_block,
    top_lower_inverse,
    top_upper_inverse,
    top_lower_block,
    top_upper_block,
    leaf_targets,
    top_targets,
):
    send, mats = call(
        prepare_kernel,
        [((FRONT, PIECE, RHS), BF), ((160, SEP), BF)],
        (
            keep(leaf_source),
            keep(top_lower_inverse),
            keep(top_upper_inverse),
            keep(jnp.swapaxes(top_lower_block, 1, 2)),
            keep(top_upper_block),
        ),
        specs=[HBM] * 5,
        scratch=[pltpu.VMEM((PIECE, RHS), F32), pltpu.SemaphoreType.DMA((6,))],
        size=1 << 20,
    )
    leaf_lower_block, send = lax.optimization_barrier((leaf_lower_block, send))
    (spread,) = call(
        spread_kernel,
        [((SPAN, PIECE), BF)],
        (leaf_lower_block, leaf_targets),
        flops=2 * UPD * SPAN * PIECE,
        size=2 << 20,
    )
    got = exchange(send, "front")
    got, mats, spread, *parts = lax.optimization_barrier((got, mats, spread, *shifts(mats, 0)))
    (mats,) = call(pack_kernel, [((4, 160, SEP), BF)], (mats, *parts), size=1 << 20)
    solved, send = call(
        leaf_forward_kernel,
        [((PIECE, RHS), F32), ((FRONT, 16, HALF), BF)],
        (got, leaf_lower_inverse, spread, top_source),
        flops=2 * RHS * (PIECE * SUB + 2 * PIECE * SPAN),
        size=4 << 20,
    )
    parts = shifts(mats, 1)
    got = exchange(send, "front")
    got, *parts = lax.optimization_barrier((got, *parts))
    ahead, second, later = call(
        assemble_kernel,
        [((SEP, SEP), BF), ((SEP, SEP), BF), ((3, SEP, SEP), BF)],
        (mats, *parts),
        size=5 << 20,
    )
    send, hot2, hot3 = call(
        top_forward_kernel,
        [((16, HALF), BF), ((SEP, SEP), BF), ((2 * SEP, SEP), BF)],
        (got, ahead, swap(ahead, 1), top_targets),
        flops=2 * 256 * SEP * SEP * 4,
        size=4 << 20,
    )
    send, second, later = lax.optimization_barrier((send, second, later))
    total, near, other = call(
        group_kernel,
        [((16, HALF), BF), ((16, SEP), BF), ((16, SEP // 2), BF)],
        (send, swap(send, 1), swap(send, 2), swap(send, 3), second, swap(second, 1), hot2),
        flops=2 * 256 * SEP * SEP * 3,
        size=2 << 20,
    )
    near, far, other = swap(near, 4), swap(total, 8), swap(other, 12)
    total, leaf_upper_block = lax.optimization_barrier((total, leaf_upper_block))
    (picked,) = call(
        pick_kernel,
        [((PIECE, SPAN), BF)],
        (leaf_upper_block, leaf_targets),
        flops=2 * UPD * SPAN * PIECE,
        size=2 << 20,
    )
    near, picked = lax.optimization_barrier((near, picked))
    (send,) = call(
        top_backward_kernel,
        [((FRONT, 16, HALF), BF)],
        (total, near, far, other, later, swap(later, 1), hot2, hot3),
        flops=2 * 256 * SEP * SEP * 9,
        size=5 << 20,
    )
    got = exchange(send, "front")
    send, own, side, last = call(
        leaf_backward_kernel,
        [((FRONT, PIECE, RHS), BF), ((96, RHS), F32), ((64, RHS), BF), ((32, RHS), BF)],
        (got, solved, picked),
        flops=2 * RHS * 2 * PIECE * SPAN,
        size=2 << 20,
    )
    near, far, other = swap(last, 4), swap(side, 8), swap(last, 12)
    got = exchange(send, "front")
    leaf_solution, top_solution = call(
        finish_kernel,
        [((1, PIECE, RHS), F32), ((7, ROWS, RHS), F32)],
        (got, leaf_upper_inverse, own, near, far, other),
        flops=2 * RHS * PIECE * SUB,
        size=2 << 20,
    )
    return leaf_solution, top_solution


def solution(mesh):
    in_specs = (
        P("leaf", "front", None),
        P(None, "front", None),
        P("leaf", "front", None),
        P("leaf", "front", None),
        P("leaf", None, "front"),
        P("leaf", "front", None),
        P(None, "front", None),
        P(None, "front", None),
        P(None, None, "front"),
        P(None, "front", None),
        P("leaf", None),
        P(),
    )
    out_specs = (P("leaf", "front", None), P(None, "front", None))
    return jax.shard_map(body, mesh=mesh, in_specs=in_specs, out_specs=out_specs, check_vma=False)
```

```python
import functools

import jax
import jax.numpy as jnp
from jax import lax
from jax.experimental import pallas as pl
from jax.experimental.pallas import tpu as pltpu
from jax.sharding import PartitionSpec as P

BF = jnp.bfloat16
F32 = jnp.float32
FRONT = 16
LEAVES = 16
SUB = 2048
SEP = 512
UPD = 1024
RHS = 128
ROWS = SEP // FRONT
SPAN = 3 * SEP
HALF = SPAN // 2
PIECE = SUB // FRONT
NT = (((1,), (1,)), ((), ()))
NN = (((1,), (0,)), ((), ()))


def dot(a, b, dims):
    return lax.dot_general(a, b, dims, preferred_element_type=F32)


def split_dot(x, w, dims):
    head = x.astype(BF).astype(F32)
    both = jnp.concatenate([head, x - head], axis=0).astype(BF)
    out = dot(both, w, dims)
    return out[:8] + out[8:]


def fold(x):
    half = x.shape[1] // 2
    return jnp.concatenate([x[:, :half], x[:, half:]], axis=0)


def unfold(x):
    return jnp.concatenate([x[:8], x[8:]], axis=1)


def one_hot(first, count, places):
    rows = lax.broadcasted_iota(jnp.int32, (count, places.shape[1]), 0) + first
    return jnp.where(rows == places, 1.0, 0.0).astype(BF)


def leaf_places(targets):
    owner = targets >> 9
    height = jnp.where(owner > 0, 1, 0) + jnp.where(owner > 2, 1, 0)
    return (height << 9) | (targets & (SEP - 1))


def ancestor_places(targets):
    return jnp.where(targets >= SEP, SEP, 0) + (targets & (SEP - 1))


def prepare_kernel(source, low_inv, up_inv, low, up, send, piece, sems):
    leaf = lax.axis_index("leaf")
    third = 3 + (leaf >> 2)
    second = 1 + (leaf >> 3)
    plans = [
        [(low_inv, third), (low_inv, second), (low_inv, 0), (up_inv, 0), (up, second - 1)],
        [(low, third - 1), (low, second - 1), (up_inv, second), (up, third - 1), (up_inv, third)],
    ]
    places = [send.at[pl.ds(i * ROWS + ROWS, ROWS)] for i in range(5)]
    start = pltpu.make_async_copy(source.at[0], piece, sems.at[5])
    start.start()
    for core, plan in enumerate(plans):

        @pl.when((leaf & 1) == core)
        def _(plan=plan):
            copies = [
                pltpu.make_async_copy(ref.at[index], place, sems.at[slot])
                for slot, ((ref, index), place) in enumerate(zip(plan, places))
            ]
            for copy in copies:
                copy.start()
            for copy in copies:
                copy.wait()

    start.wait()
    block = piece[...].astype(BF)
    send[0:ROWS, :] = jnp.concatenate([block[q * ROWS : q * ROWS + ROWS] for q in range(4)], axis=1)


def pack_kernel(own, a, b, c, early, later):
    for k, ref in enumerate((own, a, b, c)):
        early[k] = ref[0:64, :]
        later[k] = ref[64:192, :]


def origin(j, k):
    front = lax.axis_index("front")
    core = lax.axis_index("leaf") & 1
    y, x = front >> 2, front & 3
    dy = jnp.where(core == 0, j, k)
    dx = jnp.where(core == 0, k, j)
    return ((y - dy) & 3) * 4 + ((x - dx) & 3)


def assemble_kernel(skip, own, a, b, c, *outs):
    for j, ref in enumerate((own, a, b, c)):
        for k in range(4):
            rows = pl.ds(pl.multiple_of(origin(j, k) * ROWS, ROWS), ROWS)
            for i, out in enumerate(outs):
                first = (skip + i) * ROWS
                out[rows, :] = ref[k, first : first + ROWS, :]


def assemble_later_kernel(own, a, b, c, second, out):
    assemble_kernel(0, own, a, b, c, second, *[out.at[i] for i in range(3)])


def pick_kernel(block, targets, picked):
    places = leaf_places(targets[...])
    for part in range(3):
        rows = slice(part * SEP, part * SEP + SEP)
        picked[:, rows] = dot(block[0], one_hot(part * SEP, SEP, places), NT).astype(BF)


def spread_kernel(block, targets, top_targets, spread, hot2, hot3):
    leaf = lax.axis_index("leaf")
    hot2[...] = one_hot(0, SEP, top_targets[pl.ds(leaf >> 3, 1), :])
    hot3[...] = one_hot(0, 2 * SEP, ancestor_places(top_targets[pl.ds(2 + (leaf >> 2), 1), :]))
    places = leaf_places(targets[...])
    for part in range(3):
        hot = one_hot(part * SEP, SEP, places)
        spread[part * SEP : part * SEP + SEP, :] = dot(hot, block[0], NN).astype(BF)


def leaf_forward_kernel(own, a, b, c, inverse, spread, top, solved_out, send, source):
    leaf = lax.axis_index("leaf")
    front = lax.axis_index("front")
    for j, ref in enumerate((own, a, b, c)):
        for k in range(4):
            at = origin(j, k) * PIECE
            for q in range(4):
                rows = pl.ds(pl.multiple_of(at + q * ROWS, ROWS), ROWS)
                source[rows, :] = ref[k, 0:ROWS, q * RHS : q * RHS + RHS]
    solved = dot(inverse[0], source[...], NN)
    solved_out[...] = solved
    mine = jnp.concatenate(
        [
            top[0] * (1 / 16),
            top[1 + (leaf >> 3)] * (1 / 8),
            top[3 + (leaf >> 2)] * (1 / 4),
            jnp.zeros((32, RHS), F32),
        ],
        axis=0,
    ).T
    row = lax.broadcasted_iota(jnp.int32, (RHS, SPAN), 0)
    column = lax.broadcasted_iota(jnp.int32, (RHS, SPAN), 1)
    hot = jnp.where(column == ((row >> 5) << 9) + front * ROWS + (row & 31), 1.0, 0.0).astype(BF)
    total = dot(mine.astype(BF), hot, NN) - dot(solved.T.astype(BF), spread[...], NT)
    for to in range(FRONT):
        send[to] = fold(total[to * 8 : to * 8 + 8]).astype(BF)


def top_forward_kernel(got, first, swapped, hot3, send):
    leaf = lax.axis_index("leaf")
    total = got[0].astype(F32)
    for k in range(1, FRONT):
        total = total + got[k].astype(F32)
    total = unfold(total)

    def run(even, odd):
        solved3 = split_dot(total[:, 2 * SEP :], even[...], NT)
        update3 = split_dot(solved3, odd[...], NN)
        above = total[:, : 2 * SEP] - split_dot(update3, hot3[...], NT)
        send[...] = fold(jnp.concatenate([above, solved3], axis=1)).astype(BF)

    @pl.when((leaf & 1) == 0)
    def _():
        run(first, swapped)

    @pl.when((leaf & 1) == 1)
    def _():
        run(swapped, first)


def group_kernel(own, a, b, c, first, swapped, hot2, far, near, other):
    core = lax.axis_index("leaf") & 1
    total = (own[...].astype(F32) + a[...].astype(F32)) + (b[...].astype(F32) + c[...].astype(F32))
    total = unfold(total)

    def run(even, odd):
        solved2 = split_dot(total[:, SEP : 2 * SEP], even[...], NT)
        update2 = split_dot(solved2, odd[...], NN)
        target1 = total[:, :SEP] - split_dot(update2, hot2[...], NT)
        far[...] = fold(jnp.concatenate([target1, solved2, total[:, 2 * SEP :]], axis=1)).astype(BF)
        near[...] = fold(jnp.concatenate([target1, solved2], axis=1)).astype(BF)
        other[...] = fold(target1).astype(BF)

    @pl.when(core == 0)
    def _():
        run(first, swapped)

    @pl.when(core == 1)
    def _():
        run(swapped, first)


def top_backward_kernel(own, near, far, other, later, swapped, hot2, hot3, send):
    core = lax.axis_index("leaf") & 1
    part = unfold(own[...].astype(F32))
    side = unfold(near[...].astype(F32))
    total1 = part[:, :SEP] + side[:, :SEP] + unfold(far[...].astype(F32))[:, :SEP] + unfold(other[...].astype(F32))
    total2 = part[:, SEP : 2 * SEP] + side[:, SEP : 2 * SEP]
    total3 = part[:, 2 * SEP :]

    def run(first, last):
        mats = [first[0], first[1], first[2], last[0], last[1], last[2]]
        x1 = split_dot(split_dot(total1, mats[0], NT), mats[1], NT)
        picked2 = split_dot(x1, hot2[...], NN)
        x2 = split_dot(total2 - split_dot(picked2, mats[2], NT), mats[3], NT)
        picked3 = split_dot(jnp.concatenate([x1, x2], axis=1), hot3[...], NN)
        x3 = split_dot(total3 - split_dot(picked3, mats[4], NT), mats[5], NT)
        out = fold(jnp.concatenate([x1, x2, x3], axis=1)).astype(BF)
        for to in range(FRONT):
            send[to] = out

    @pl.when(core == 0)
    def _():
        run(later, swapped)

    @pl.when(core == 1)
    def _():
        run(swapped, later)


def leaf_backward_kernel(got, solved, picked, send, own, side, last):
    front = lax.axis_index("front")
    full = jnp.concatenate([unfold(got[k].astype(F32)) for k in range(FRONT)], axis=0).astype(BF)
    residue = (solved[...] - dot(picked[...], full, NT)).astype(BF)
    for to in range(FRONT):
        send[to] = residue
    row = lax.broadcasted_iota(jnp.int32, (96, SPAN), 0)
    column = lax.broadcasted_iota(jnp.int32, (96, SPAN), 1)
    pick = jnp.where(column == ((row >> 5) << 9) + front * ROWS + (row & 31), 1.0, 0.0).astype(BF)
    rows = dot(pick, full, NT)
    own[...] = rows
    side[...] = rows[32:96, :].astype(BF)
    last[...] = rows[64:96, :].astype(BF)


def finish_kernel(got, inverse, own, near, far, other, leaf_out, top_out):
    leaf = lax.axis_index("leaf")
    leaf_out[0] = dot(inverse[0], got[...].reshape(SUB, RHS), NN)
    second = leaf >> 3
    third = leaf >> 2
    top_out[0] = own[0:32, :]
    top_out[1 + second] = own[32:64, :]
    top_out[1 + (second ^ 1)] = far[0:32, :].astype(F32)
    top_out[3 + third] = own[64:96, :]
    top_out[3 + (third ^ 1)] = near[...].astype(F32)
    top_out[3 + (third ^ 2)] = far[32:64, :].astype(F32)
    top_out[3 + (third ^ 3)] = other[...].astype(F32)


VMEM = pl.BlockSpec(memory_space=pltpu.VMEM)
HBM = pl.BlockSpec(memory_space=pltpu.HBM)


def keep(x):
    return pltpu.with_memory_space_constraint(x, pltpu.HBM)


def call(kernel, outs, args, specs=None, scratch=(), flops=0, size=0):
    shapes = [jax.ShapeDtypeStruct(shape, kind) for shape, kind in outs]
    return pl.pallas_call(
        kernel,
        out_shape=shapes,
        in_specs=specs or [VMEM] * len(args),
        out_specs=[VMEM] * len(shapes),
        scratch_shapes=list(scratch),
        compiler_params=pltpu.CompilerParams(vmem_limit_bytes=16 * 1024 * 1024),
        cost_estimate=pl.CostEstimate(flops=flops, bytes_accessed=size, transcendentals=0),
    )(*args)


def swap(x, flip):
    return lax.ppermute(x, "leaf", [(i, i ^ flip) for i in range(LEAVES)])


def shifts(x, turn):
    def moved(leaf, front, k):
        y, x = front // 4, front % 4
        if (leaf + turn) % 2 == 0:
            return leaf * FRONT + y * 4 + (x + k) % 4
        return leaf * FRONT + (y + k) % 4 * 4 + x

    everyone = [(leaf, front) for leaf in range(LEAVES) for front in range(FRONT)]
    return [
        lax.ppermute(x, ("leaf", "front"), [(leaf * FRONT + front, moved(leaf, front, k)) for leaf, front in everyone])
        for k in (1, 2, 3)
    ]


def exchange(x, axis, groups=None):
    return lax.all_to_all(x, axis, 0, 0, tiled=True, axis_index_groups=groups)


def body(
    leaf_source,
    top_source,
    leaf_lower_inverse,
    leaf_upper_inverse,
    leaf_lower_block,
    leaf_upper_block,
    top_lower_inverse,
    top_upper_inverse,
    top_lower_block,
    top_upper_block,
    leaf_targets,
    top_targets,
):
    (send,) = call(
        prepare_kernel,
        [((192, SEP), BF)],
        (
            keep(leaf_source),
            keep(top_lower_inverse),
            keep(top_upper_inverse),
            keep(jnp.swapaxes(top_lower_block, 1, 2)),
            keep(top_upper_block),
        ),
        specs=[HBM] * 5,
        scratch=[pltpu.VMEM((PIECE, RHS), F32), pltpu.SemaphoreType.DMA((6,))],
        size=1 << 20,
    )
    early, later = call(
        pack_kernel,
        [((4, 64, SEP), BF), ((4, 128, SEP), BF)],
        (send, *shifts(send, 0)),
        size=1 << 20,
    )
    parts = shifts(early, 1)
    send, leaf_lower_block = lax.optimization_barrier((send, leaf_lower_block))
    spread, hot2, hot3 = call(
        spread_kernel,
        [((SPAN, PIECE), BF), ((SEP, SEP), BF), ((2 * SEP, SEP), BF)],
        (leaf_lower_block, leaf_targets, top_targets),
        flops=2 * UPD * SPAN * PIECE,
        size=2 << 20,
    )
    later, spread, *parts = lax.optimization_barrier((later, spread, *parts))
    (ahead,) = call(functools.partial(assemble_kernel, 1), [((SEP, SEP), BF)], (early, *parts), size=1 << 20)
    swapped = swap(ahead, 1)
    solved, send = call(
        leaf_forward_kernel,
        [((PIECE, RHS), F32), ((FRONT, 16, HALF), BF)],
        (early, *parts, leaf_lower_inverse, spread, top_source),
        scratch=[pltpu.VMEM((SUB, RHS), BF)],
        flops=2 * RHS * (PIECE * SUB + UPD * PIECE + UPD * SPAN),
        size=4 << 20,
    )
    parts = shifts(later, 1)
    got = exchange(send, "front")
    got, *parts = lax.optimization_barrier((got, *parts))
    second, later = call(
        assemble_later_kernel, [((SEP, SEP), BF), ((3, SEP, SEP), BF)], (later, *parts), size=4 << 20
    )
    (send,) = call(
        top_forward_kernel,
        [((16, HALF), BF)],
        (got, ahead, swapped, hot3),
        flops=2 * 256 * SEP * SEP * 4,
        size=4 << 20,
    )
    send, second, later = lax.optimization_barrier((send, second, later))
    total, near, other = call(
        group_kernel,
        [((16, HALF), BF), ((16, SEP), BF), ((16, SEP // 2), BF)],
        (send, swap(send, 1), swap(send, 2), swap(send, 3), second, swap(second, 1), hot2),
        flops=2 * 256 * SEP * SEP * 3,
        size=2 << 20,
    )
    near, far, other = swap(near, 4), swap(total, 8), swap(other, 12)
    total, leaf_upper_block = lax.optimization_barrier((total, leaf_upper_block))
    (picked,) = call(
        pick_kernel,
        [((PIECE, SPAN), BF)],
        (leaf_upper_block, leaf_targets),
        flops=2 * UPD * SPAN * PIECE,
        size=2 << 20,
    )
    near, picked = lax.optimization_barrier((near, picked))
    (send,) = call(
        top_backward_kernel,
        [((FRONT, 16, HALF), BF)],
        (total, near, far, other, later, swap(later, 1), hot2, hot3),
        flops=2 * 256 * SEP * SEP * 9,
        size=5 << 20,
    )
    got = exchange(send, "front")
    send, own, side, last = call(
        leaf_backward_kernel,
        [((FRONT, PIECE, RHS), BF), ((96, RHS), F32), ((64, RHS), BF), ((32, RHS), BF)],
        (got, solved, picked),
        flops=2 * RHS * 2 * PIECE * SPAN,
        size=2 << 20,
    )
    near, far, other = swap(last, 4), swap(side, 8), swap(last, 12)
    got = exchange(send, "front")
    leaf_solution, top_solution = call(
        finish_kernel,
        [((1, PIECE, RHS), F32), ((7, ROWS, RHS), F32)],
        (got, leaf_upper_inverse, own, near, far, other),
        flops=2 * RHS * PIECE * SUB,
        size=2 << 20,
    )
    return leaf_solution, top_solution


def solution(mesh):
    in_specs = (
        P("leaf", "front", None),
        P(None, "front", None),
        P("leaf", "front", None),
        P("leaf", "front", None),
        P("leaf", None, "front"),
        P("leaf", "front", None),
        P(None, "front", None),
        P(None, "front", None),
        P(None, None, "front"),
        P(None, "front", None),
        P("leaf", None),
        P(),
    )
    out_specs = (P("leaf", "front", None), P(None, "front", None))
    return jax.shard_map(body, mesh=mesh, in_specs=in_specs, out_specs=out_specs, check_vma=False)
```

```python
import functools

import jax
import jax.numpy as jnp
from jax import lax
from jax.experimental import pallas as pl
from jax.experimental.pallas import tpu as pltpu
from jax.sharding import PartitionSpec as P

BF = jnp.bfloat16
F32 = jnp.float32
FRONT = 16
LEAVES = 16
SUB = 2048
SEP = 512
UPD = 1024
RHS = 128
ROWS = SEP // FRONT
SPAN = 3 * SEP
HALF = SPAN // 2
PIECE = SUB // FRONT
NT = (((1,), (1,)), ((), ()))
NN = (((1,), (0,)), ((), ()))


def dot(a, b, dims):
    return lax.dot_general(a, b, dims, preferred_element_type=F32)


def split_dot(x, w, dims):
    head = x.astype(BF).astype(F32)
    both = jnp.concatenate([head, x - head], axis=0).astype(BF)
    out = dot(both, w, dims)
    return out[:8] + out[8:]


def fold(x):
    half = x.shape[1] // 2
    return jnp.concatenate([x[:, :half], x[:, half:]], axis=0)


def unfold(x):
    return jnp.concatenate([x[:8], x[8:]], axis=1)


def one_hot(first, count, places):
    rows = lax.broadcasted_iota(jnp.int32, (count, places.shape[1]), 0) + first
    return jnp.where(rows == places, 1.0, 0.0).astype(BF)


def leaf_places(targets):
    owner = targets >> 9
    height = jnp.where(owner > 0, 1, 0) + jnp.where(owner > 2, 1, 0)
    return (height << 9) | (targets & (SEP - 1))


def ancestor_places(targets):
    return jnp.where(targets >= SEP, SEP, 0) + (targets & (SEP - 1))


def prepare_kernel(source, low_inv, up_inv, low, up, send, piece, sems):
    leaf = lax.axis_index("leaf")
    third = 3 + (leaf >> 2)
    second = 1 + (leaf >> 3)
    plans = [
        [(low_inv, third), (low_inv, second), (low_inv, 0), (up_inv, 0), (up, second - 1)],
        [(low, third - 1), (low, second - 1), (up_inv, second), (up, third - 1), (up_inv, third)],
    ]
    places = [send.at[pl.ds(i * ROWS + ROWS, ROWS)] for i in range(5)]
    start = pltpu.make_async_copy(source.at[0], piece, sems.at[5])
    start.start()
    for core, plan in enumerate(plans):

        @pl.when((leaf & 1) == core)
        def _(plan=plan):
            copies = [
                pltpu.make_async_copy(ref.at[index], place, sems.at[slot])
                for slot, ((ref, index), place) in enumerate(zip(plan, places))
            ]
            for copy in copies:
                copy.start()
            for copy in copies:
                copy.wait()

    start.wait()
    block = piece[...].astype(BF)
    send[0:ROWS, :] = jnp.concatenate([block[q * ROWS : q * ROWS + ROWS] for q in range(4)], axis=1)


def pack_kernel(own, a, b, c, early, later):
    for k, ref in enumerate((own, a, b, c)):
        early[k] = ref[0:64, :]
        later[k] = ref[64:192, :]


def origin(j, k):
    front = lax.axis_index("front")
    core = lax.axis_index("leaf") & 1
    y, x = front >> 2, front & 3
    dy = jnp.where(core == 0, j, k)
    dx = jnp.where(core == 0, k, j)
    return ((y - dy) & 3) * 4 + ((x - dx) & 3)


def assemble_kernel(skip, own, a, b, c, *outs):
    for j, ref in enumerate((own, a, b, c)):
        for k in range(4):
            rows = pl.ds(pl.multiple_of(origin(j, k) * ROWS, ROWS), ROWS)
            for i, out in enumerate(outs):
                first = (skip + i) * ROWS
                out[rows, :] = ref[k, first : first + ROWS, :]


def assemble_later_kernel(own, a, b, c, second, out):
    assemble_kernel(0, own, a, b, c, second, *[out.at[i] for i in range(3)])


def pick_kernel(block, targets, picked):
    places = leaf_places(targets[...])
    for part in range(3):
        rows = slice(part * SEP, part * SEP + SEP)
        picked[:, rows] = dot(block[0], one_hot(part * SEP, SEP, places), NT).astype(BF)


def spread_kernel(block, targets, top_targets, spread, hot2, hot3):
    leaf = lax.axis_index("leaf")
    hot2[...] = one_hot(0, SEP, top_targets[pl.ds(leaf >> 3, 1), :])
    hot3[...] = one_hot(0, 2 * SEP, ancestor_places(top_targets[pl.ds(2 + (leaf >> 2), 1), :]))
    places = leaf_places(targets[...])
    for part in range(3):
        hot = one_hot(part * SEP, SEP, places)
        spread[part * SEP : part * SEP + SEP, :] = dot(hot, block[0], NN).astype(BF)


def leaf_forward_kernel(own, a, b, c, inverse, spread, top, solved_out, send, source):
    leaf = lax.axis_index("leaf")
    front = lax.axis_index("front")
    for j, ref in enumerate((own, a, b, c)):
        for k in range(4):
            at = origin(j, k) * PIECE
            for q in range(4):
                rows = pl.ds(pl.multiple_of(at + q * ROWS, ROWS), ROWS)
                source[rows, :] = ref[k, 0:ROWS, q * RHS : q * RHS + RHS]
    solved = dot(inverse[0], source[...], NN)
    solved_out[...] = solved
    mine = jnp.concatenate(
        [
            top[0] * (1 / 16),
            top[1 + (leaf >> 3)] * (1 / 8),
            top[3 + (leaf >> 2)] * (1 / 4),
            jnp.zeros((32, RHS), F32),
        ],
        axis=0,
    ).T
    row = lax.broadcasted_iota(jnp.int32, (RHS, SPAN), 0)
    column = lax.broadcasted_iota(jnp.int32, (RHS, SPAN), 1)
    hot = jnp.where(column == ((row >> 5) << 9) + front * ROWS + (row & 31), 1.0, 0.0).astype(BF)
    total = dot(mine.astype(BF), hot, NN) - dot(solved.T.astype(BF), spread[...], NT)
    for to in range(FRONT):
        send[to] = fold(total[to * 8 : to * 8 + 8]).astype(BF)


def top_forward_kernel(got, first, swapped, hot3, send):
    leaf = lax.axis_index("leaf")
    total = got[0].astype(F32)
    for k in range(1, FRONT):
        total = total + got[k].astype(F32)
    total = unfold(total)

    def run(even, odd):
        solved3 = split_dot(total[:, 2 * SEP :], even[...], NT)
        update3 = split_dot(solved3, odd[...], NN)
        above = total[:, : 2 * SEP] - split_dot(update3, hot3[...], NT)
        send[...] = fold(jnp.concatenate([above, solved3], axis=1)).astype(BF)

    @pl.when((leaf & 1) == 0)
    def _():
        run(first, swapped)

    @pl.when((leaf & 1) == 1)
    def _():
        run(swapped, first)


def group_kernel(own, a, b, c, first, swapped, hot2, far, near, other):
    core = lax.axis_index("leaf") & 1
    total = (own[...].astype(F32) + a[...].astype(F32)) + (b[...].astype(F32) + c[...].astype(F32))
    total = unfold(total)

    def run(even, odd):
        solved2 = split_dot(total[:, SEP : 2 * SEP], even[...], NT)
        update2 = split_dot(solved2, odd[...], NN)
        target1 = total[:, :SEP] - split_dot(update2, hot2[...], NT)
        far[...] = fold(jnp.concatenate([target1, solved2, total[:, 2 * SEP :]], axis=1)).astype(BF)
        near[...] = fold(jnp.concatenate([target1, solved2], axis=1)).astype(BF)
        other[...] = fold(target1).astype(BF)

    @pl.when(core == 0)
    def _():
        run(first, swapped)

    @pl.when(core == 1)
    def _():
        run(swapped, first)


def top_backward_kernel(own, near, far, other, later, swapped, hot2, hot3, send):
    core = lax.axis_index("leaf") & 1
    part = unfold(own[...].astype(F32))
    side = unfold(near[...].astype(F32))
    total1 = part[:, :SEP] + side[:, :SEP] + unfold(far[...].astype(F32))[:, :SEP] + unfold(other[...].astype(F32))
    total2 = part[:, SEP : 2 * SEP] + side[:, SEP : 2 * SEP]
    total3 = part[:, 2 * SEP :]

    def run(first, last):
        mats = [first[0], first[1], first[2], last[0], last[1], last[2]]
        x1 = split_dot(split_dot(total1, mats[0], NT), mats[1], NT)
        picked2 = split_dot(x1, hot2[...], NN)
        x2 = split_dot(total2 - split_dot(picked2, mats[2], NT), mats[3], NT)
        picked3 = split_dot(jnp.concatenate([x1, x2], axis=1), hot3[...], NN)
        x3 = split_dot(total3 - split_dot(picked3, mats[4], NT), mats[5], NT)
        out = fold(jnp.concatenate([x1, x2, x3], axis=1)).astype(BF)
        for to in range(FRONT):
            send[to] = out

    @pl.when(core == 0)
    def _():
        run(later, swapped)

    @pl.when(core == 1)
    def _():
        run(swapped, later)


def leaf_backward_kernel(got, solved, picked, send, own, side, last):
    front = lax.axis_index("front")
    full = jnp.concatenate([unfold(got[k].astype(F32)) for k in range(FRONT)], axis=0).astype(BF)
    residue = (solved[...] - dot(picked[...], full, NT)).astype(BF)
    for to in range(FRONT):
        send[to] = residue
    row = lax.broadcasted_iota(jnp.int32, (96, SPAN), 0)
    column = lax.broadcasted_iota(jnp.int32, (96, SPAN), 1)
    pick = jnp.where(column == ((row >> 5) << 9) + front * ROWS + (row & 31), 1.0, 0.0).astype(BF)
    rows = dot(pick, full, NT)
    own[...] = rows
    side[...] = rows[32:96, :].astype(BF)
    last[...] = rows[64:96, :].astype(BF)


def finish_kernel(got, inverse, own, near, far, other, leaf_out, top_out):
    leaf = lax.axis_index("leaf")
    leaf_out[0] = dot(inverse[0], got[...].reshape(SUB, RHS), NN)
    second = leaf >> 3
    third = leaf >> 2
    top_out[0] = own[0:32, :]
    top_out[1 + second] = own[32:64, :]
    top_out[1 + (second ^ 1)] = far[0:32, :].astype(F32)
    top_out[3 + third] = own[64:96, :]
    top_out[3 + (third ^ 1)] = near[...].astype(F32)
    top_out[3 + (third ^ 2)] = far[32:64, :].astype(F32)
    top_out[3 + (third ^ 3)] = other[...].astype(F32)


VMEM = pl.BlockSpec(memory_space=pltpu.VMEM)
HBM = pl.BlockSpec(memory_space=pltpu.HBM)


def keep(x):
    return pltpu.with_memory_space_constraint(x, pltpu.HBM)


def call(kernel, outs, args, specs=None, scratch=(), flops=0, size=0):
    shapes = [jax.ShapeDtypeStruct(shape, kind) for shape, kind in outs]
    return pl.pallas_call(
        kernel,
        out_shape=shapes,
        in_specs=specs or [VMEM] * len(args),
        out_specs=[VMEM] * len(shapes),
        scratch_shapes=list(scratch),
        compiler_params=pltpu.CompilerParams(vmem_limit_bytes=16 * 1024 * 1024),
        cost_estimate=pl.CostEstimate(flops=flops, bytes_accessed=size, transcendentals=0),
    )(*args)


def swap(x, flip):
    return lax.ppermute(x, "leaf", [(i, i ^ flip) for i in range(LEAVES)])


def shifts(x, turn):
    def moved(leaf, front, k):
        y, x = front // 4, front % 4
        if (leaf + turn) % 2 == 0:
            return leaf * FRONT + y * 4 + (x + k) % 4
        return leaf * FRONT + (y + k) % 4 * 4 + x

    everyone = [(leaf, front) for leaf in range(LEAVES) for front in range(FRONT)]
    return [
        lax.ppermute(x, ("leaf", "front"), [(leaf * FRONT + front, moved(leaf, front, k)) for leaf, front in everyone])
        for k in (1, 2, 3)
    ]


def exchange(x, axis, groups=None):
    return lax.all_to_all(x, axis, 0, 0, tiled=True, axis_index_groups=groups)


def body(
    leaf_source,
    top_source,
    leaf_lower_inverse,
    leaf_upper_inverse,
    leaf_lower_block,
    leaf_upper_block,
    top_lower_inverse,
    top_upper_inverse,
    top_lower_block,
    top_upper_block,
    leaf_targets,
    top_targets,
):
    (send,) = call(
        prepare_kernel,
        [((192, SEP), BF)],
        (
            keep(leaf_source),
            keep(top_lower_inverse),
            keep(top_upper_inverse),
            keep(jnp.swapaxes(top_lower_block, 1, 2)),
            keep(top_upper_block),
        ),
        specs=[HBM] * 5,
        scratch=[pltpu.VMEM((PIECE, RHS), F32), pltpu.SemaphoreType.DMA((6,))],
        size=1 << 20,
    )
    early, later = call(
        pack_kernel,
        [((4, 64, SEP), BF), ((4, 128, SEP), BF)],
        (send, *shifts(send, 0)),
        size=1 << 20,
    )
    parts = shifts(early, 1)
    send, leaf_lower_block = lax.optimization_barrier((send, leaf_lower_block))
    spread, hot2, hot3 = call(
        spread_kernel,
        [((SPAN, PIECE), BF), ((SEP, SEP), BF), ((2 * SEP, SEP), BF)],
        (leaf_lower_block, leaf_targets, top_targets),
        flops=2 * UPD * SPAN * PIECE,
        size=2 << 20,
    )
    spread, *parts = lax.optimization_barrier((spread, *parts))
    (ahead,) = call(functools.partial(assemble_kernel, 1), [((SEP, SEP), BF)], (early, *parts), size=1 << 20)
    swapped = swap(ahead, 1)
    solved, send = call(
        leaf_forward_kernel,
        [((PIECE, RHS), F32), ((FRONT, 16, HALF), BF)],
        (early, *parts, leaf_lower_inverse, spread, top_source),
        scratch=[pltpu.VMEM((SUB, RHS), BF)],
        flops=2 * RHS * (PIECE * SUB + UPD * PIECE + UPD * SPAN),
        size=4 << 20,
    )
    parts = shifts(later, 1)
    got = exchange(send, "front")
    got, *parts = lax.optimization_barrier((got, *parts))
    second, later = call(
        assemble_later_kernel, [((SEP, SEP), BF), ((3, SEP, SEP), BF)], (later, *parts), size=4 << 20
    )
    (send,) = call(
        top_forward_kernel,
        [((16, HALF), BF)],
        (got, ahead, swapped, hot3),
        flops=2 * 256 * SEP * SEP * 4,
        size=4 << 20,
    )
    send, second, later = lax.optimization_barrier((send, second, later))
    total, near, other = call(
        group_kernel,
        [((16, HALF), BF), ((16, SEP), BF), ((16, SEP // 2), BF)],
        (send, swap(send, 1), swap(send, 2), swap(send, 3), second, swap(second, 1), hot2),
        flops=2 * 256 * SEP * SEP * 3,
        size=2 << 20,
    )
    near, far, other = swap(near, 4), swap(total, 8), swap(other, 12)
    total, leaf_upper_block = lax.optimization_barrier((total, leaf_upper_block))
    (picked,) = call(
        pick_kernel,
        [((PIECE, SPAN), BF)],
        (leaf_upper_block, leaf_targets),
        flops=2 * UPD * SPAN * PIECE,
        size=2 << 20,
    )
    near, picked = lax.optimization_barrier((near, picked))
    (send,) = call(
        top_backward_kernel,
        [((FRONT, 16, HALF), BF)],
        (total, near, far, other, later, swap(later, 1), hot2, hot3),
        flops=2 * 256 * SEP * SEP * 9,
        size=5 << 20,
    )
    got = exchange(send, "front")
    send, own, side, last = call(
        leaf_backward_kernel,
        [((FRONT, PIECE, RHS), BF), ((96, RHS), F32), ((64, RHS), BF), ((32, RHS), BF)],
        (got, solved, picked),
        flops=2 * RHS * 2 * PIECE * SPAN,
        size=2 << 20,
    )
    near, far, other = swap(last, 4), swap(side, 8), swap(last, 12)
    got = exchange(send, "front")
    leaf_solution, top_solution = call(
        finish_kernel,
        [((1, PIECE, RHS), F32), ((7, ROWS, RHS), F32)],
        (got, leaf_upper_inverse, own, near, far, other),
        flops=2 * RHS * PIECE * SUB,
        size=2 << 20,
    )
    return leaf_solution, top_solution


def solution(mesh):
    in_specs = (
        P("leaf", "front", None),
        P(None, "front", None),
        P("leaf", "front", None),
        P("leaf", "front", None),
        P("leaf", None, "front"),
        P("leaf", "front", None),
        P(None, "front", None),
        P(None, "front", None),
        P(None, None, "front"),
        P(None, "front", None),
        P("leaf", None),
        P(),
    )
    out_specs = (P("leaf", "front", None), P(None, "front", None))
    return jax.shard_map(body, mesh=mesh, in_specs=in_specs, out_specs=out_specs, check_vma=False)
```

```python
import functools

import jax
import jax.numpy as jnp
from jax import lax
from jax.experimental import pallas as pl
from jax.experimental.pallas import tpu as pltpu
from jax.sharding import PartitionSpec as P

BF = jnp.bfloat16
F32 = jnp.float32
FRONT = 16
LEAVES = 16
SUB = 2048
SEP = 512
UPD = 1024
RHS = 128
ROWS = SEP // FRONT
SPAN = 3 * SEP
HALF = SPAN // 2
PIECE = SUB // FRONT
NT = (((1,), (1,)), ((), ()))
NN = (((1,), (0,)), ((), ()))


def dot(a, b, dims):
    return lax.dot_general(a, b, dims, preferred_element_type=F32)


def split_dot(x, w, dims):
    head = x.astype(BF).astype(F32)
    both = jnp.concatenate([head, x - head], axis=0).astype(BF)
    out = dot(both, w, dims)
    return out[:8] + out[8:]


def fold(x):
    half = x.shape[1] // 2
    return jnp.concatenate([x[:, :half], x[:, half:]], axis=0)


def unfold(x):
    return jnp.concatenate([x[:8], x[8:]], axis=1)


def one_hot(first, count, places):
    rows = lax.broadcasted_iota(jnp.int32, (count, places.shape[1]), 0) + first
    return jnp.where(rows == places, 1.0, 0.0).astype(BF)


def leaf_places(targets):
    owner = targets >> 9
    height = jnp.where(owner > 0, 1, 0) + jnp.where(owner > 2, 1, 0)
    return (height << 9) | (targets & (SEP - 1))


def ancestor_places(targets):
    return jnp.where(targets >= SEP, SEP, 0) + (targets & (SEP - 1))


def prepare_kernel(source, low_inv, up_inv, low, up, send, piece, sems):
    leaf = lax.axis_index("leaf")
    third = 3 + (leaf >> 2)
    second = 1 + (leaf >> 3)
    plans = [
        [(low_inv, third), (low_inv, second), (low_inv, 0), (up_inv, 0), (up, second - 1)],
        [(low, third - 1), (low, second - 1), (up_inv, second), (up, third - 1), (up_inv, third)],
    ]
    places = [send.at[pl.ds(i * ROWS + ROWS, ROWS)] for i in range(5)]
    start = pltpu.make_async_copy(source.at[0], piece, sems.at[5])
    start.start()
    for core, plan in enumerate(plans):

        @pl.when((leaf & 1) == core)
        def _(plan=plan):
            copies = [
                pltpu.make_async_copy(ref.at[index], place, sems.at[slot])
                for slot, ((ref, index), place) in enumerate(zip(plan, places))
            ]
            for copy in copies:
                copy.start()
            for copy in copies:
                copy.wait()

    start.wait()
    block = piece[...].astype(BF)
    send[0:ROWS, :] = jnp.concatenate([block[q * ROWS : q * ROWS + ROWS] for q in range(4)], axis=1)


def pack_kernel(own, a, b, c, early, later):
    for k, ref in enumerate((own, a, b, c)):
        early[k] = ref[0:64, :]
        later[k] = ref[64:192, :]


def origin(j, k):
    front = lax.axis_index("front")
    core = lax.axis_index("leaf") & 1
    y, x = front >> 2, front & 3
    dy = jnp.where(core == 0, j, k)
    dx = jnp.where(core == 0, k, j)
    return ((y - dy) & 3) * 4 + ((x - dx) & 3)


def assemble_kernel(skip, own, a, b, c, *outs):
    for j, ref in enumerate((own, a, b, c)):
        for k in range(4):
            rows = pl.ds(pl.multiple_of(origin(j, k) * ROWS, ROWS), ROWS)
            for i, out in enumerate(outs):
                first = (skip + i) * ROWS
                out[rows, :] = ref[k, first : first + ROWS, :]


def assemble_later_kernel(own, a, b, c, second, out):
    assemble_kernel(0, own, a, b, c, second, *[out.at[i] for i in range(3)])


def pick_kernel(block, targets, picked):
    places = leaf_places(targets[...])
    for part in range(3):
        rows = slice(part * SEP, part * SEP + SEP)
        picked[:, rows] = dot(block[0], one_hot(part * SEP, SEP, places), NT).astype(BF)


def spread_kernel(block, targets, top_targets, spread, hot2, hot3):
    leaf = lax.axis_index("leaf")
    hot2[...] = one_hot(0, SEP, top_targets[pl.ds(leaf >> 3, 1), :])
    hot3[...] = one_hot(0, 2 * SEP, ancestor_places(top_targets[pl.ds(2 + (leaf >> 2), 1), :]))
    places = leaf_places(targets[...])
    for part in range(3):
        hot = one_hot(part * SEP, SEP, places)
        spread[part * SEP : part * SEP + SEP, :] = dot(hot, block[0], NN).astype(BF)


def leaf_forward_kernel(own, a, b, c, inverse, spread, top, solved_out, send, source, held, sem):
    leaf = lax.axis_index("leaf")
    front = lax.axis_index("front")
    for j, ref in enumerate((own, a, b, c)):
        for k in range(4):
            at = origin(j, k) * PIECE
            for q in range(4):
                rows = pl.ds(pl.multiple_of(at + q * ROWS, ROWS), ROWS)
                source[rows, :] = ref[k, 0:ROWS, q * RHS : q * RHS + RHS]
    solved = dot(inverse[0], source[...], NN)
    held[...] = solved
    copy = pltpu.make_async_copy(held, solved_out, sem)
    copy.start()
    mine = jnp.concatenate(
        [
            top[0] * (1 / 16),
            top[1 + (leaf >> 3)] * (1 / 8),
            top[3 + (leaf >> 2)] * (1 / 4),
            jnp.zeros((32, RHS), F32),
        ],
        axis=0,
    ).T
    row = lax.broadcasted_iota(jnp.int32, (RHS, SPAN), 0)
    column = lax.broadcasted_iota(jnp.int32, (RHS, SPAN), 1)
    hot = jnp.where(column == ((row >> 5) << 9) + front * ROWS + (row & 31), 1.0, 0.0).astype(BF)
    total = dot(mine.astype(BF), hot, NN) - dot(solved.T.astype(BF), spread[...], NT)
    for to in range(FRONT):
        send[to] = fold(total[to * 8 : to * 8 + 8]).astype(BF)
    copy.wait()


def top_forward_kernel(got, first, swapped, hot3, send):
    leaf = lax.axis_index("leaf")
    total = got[0].astype(F32)
    for k in range(1, FRONT):
        total = total + got[k].astype(F32)
    total = unfold(total)

    def run(even, odd):
        solved3 = split_dot(total[:, 2 * SEP :], even[...], NT)
        update3 = split_dot(solved3, odd[...], NN)
        above = total[:, : 2 * SEP] - split_dot(update3, hot3[...], NT)
        send[...] = fold(jnp.concatenate([above, solved3], axis=1)).astype(BF)

    @pl.when((leaf & 1) == 0)
    def _():
        run(first, swapped)

    @pl.when((leaf & 1) == 1)
    def _():
        run(swapped, first)


def group_kernel(own, a, b, c, first, swapped, hot2, far, near, other):
    core = lax.axis_index("leaf") & 1
    total = (own[...].astype(F32) + a[...].astype(F32)) + (b[...].astype(F32) + c[...].astype(F32))
    total = unfold(total)

    def run(even, odd):
        solved2 = split_dot(total[:, SEP : 2 * SEP], even[...], NT)
        update2 = split_dot(solved2, odd[...], NN)
        target1 = total[:, :SEP] - split_dot(update2, hot2[...], NT)
        far[...] = fold(jnp.concatenate([target1, solved2, total[:, 2 * SEP :]], axis=1)).astype(BF)
        near[...] = fold(jnp.concatenate([target1, solved2], axis=1)).astype(BF)
        other[...] = fold(target1).astype(BF)

    @pl.when(core == 0)
    def _():
        run(first, swapped)

    @pl.when(core == 1)
    def _():
        run(swapped, first)


def top_backward_kernel(own, near, far, other, later, swapped, hot2, hot3, send):
    core = lax.axis_index("leaf") & 1
    part = unfold(own[...].astype(F32))
    side = unfold(near[...].astype(F32))
    total1 = part[:, :SEP] + side[:, :SEP] + unfold(far[...].astype(F32))[:, :SEP] + unfold(other[...].astype(F32))
    total2 = part[:, SEP : 2 * SEP] + side[:, SEP : 2 * SEP]
    total3 = part[:, 2 * SEP :]

    def run(first, last):
        mats = [first[0], first[1], first[2], last[0], last[1], last[2]]
        x1 = split_dot(split_dot(total1, mats[0], NT), mats[1], NT)
        picked2 = split_dot(x1, hot2[...], NN)
        x2 = split_dot(total2 - split_dot(picked2, mats[2], NT), mats[3], NT)
        picked3 = split_dot(jnp.concatenate([x1, x2], axis=1), hot3[...], NN)
        x3 = split_dot(total3 - split_dot(picked3, mats[4], NT), mats[5], NT)
        out = fold(jnp.concatenate([x1, x2, x3], axis=1)).astype(BF)
        for to in range(FRONT):
            send[to] = out

    @pl.when(core == 0)
    def _():
        run(later, swapped)

    @pl.when(core == 1)
    def _():
        run(swapped, later)


def leaf_backward_kernel(got, solved, picked, send, own, side, last, held, sem):
    copy = pltpu.make_async_copy(solved, held, sem)
    copy.start()
    front = lax.axis_index("front")
    full = jnp.concatenate([unfold(got[k].astype(F32)) for k in range(FRONT)], axis=0).astype(BF)
    change = dot(picked[...], full, NT)
    copy.wait()
    residue = (held[...] - change).astype(BF)
    for to in range(FRONT):
        send[to] = residue
    row = lax.broadcasted_iota(jnp.int32, (96, SPAN), 0)
    column = lax.broadcasted_iota(jnp.int32, (96, SPAN), 1)
    pick = jnp.where(column == ((row >> 5) << 9) + front * ROWS + (row & 31), 1.0, 0.0).astype(BF)
    rows = dot(pick, full, NT)
    own[...] = rows
    side[...] = rows[32:96, :].astype(BF)
    last[...] = rows[64:96, :].astype(BF)


def finish_kernel(got, inverse, own, near, far, other, leaf_out, top_out):
    leaf = lax.axis_index("leaf")
    leaf_out[0] = dot(inverse[0], got[...].reshape(SUB, RHS), NN)
    second = leaf >> 3
    third = leaf >> 2
    top_out[0] = own[0:32, :]
    top_out[1 + second] = own[32:64, :]
    top_out[1 + (second ^ 1)] = far[0:32, :].astype(F32)
    top_out[3 + third] = own[64:96, :]
    top_out[3 + (third ^ 1)] = near[...].astype(F32)
    top_out[3 + (third ^ 2)] = far[32:64, :].astype(F32)
    top_out[3 + (third ^ 3)] = other[...].astype(F32)


VMEM = pl.BlockSpec(memory_space=pltpu.VMEM)
HBM = pl.BlockSpec(memory_space=pltpu.HBM)


def keep(x):
    return pltpu.with_memory_space_constraint(x, pltpu.HBM)


def call(kernel, outs, args, specs=None, out_specs=None, scratch=(), flops=0, size=0):
    shapes = [jax.ShapeDtypeStruct(*out) if isinstance(out, tuple) else out for out in outs]
    return pl.pallas_call(
        kernel,
        out_shape=shapes,
        in_specs=specs or [VMEM] * len(args),
        out_specs=out_specs or [VMEM] * len(shapes),
        scratch_shapes=list(scratch),
        compiler_params=pltpu.CompilerParams(vmem_limit_bytes=16 * 1024 * 1024),
        cost_estimate=pl.CostEstimate(flops=flops, bytes_accessed=size, transcendentals=0),
    )(*args)


def swap(x, flip):
    return lax.ppermute(x, "leaf", [(i, i ^ flip) for i in range(LEAVES)])


def shifts(x, turn):
    def moved(leaf, front, k):
        y, x = front // 4, front % 4
        if (leaf + turn) % 2 == 0:
            return leaf * FRONT + y * 4 + (x + k) % 4
        return leaf * FRONT + (y + k) % 4 * 4 + x

    everyone = [(leaf, front) for leaf in range(LEAVES) for front in range(FRONT)]
    return [
        lax.ppermute(x, ("leaf", "front"), [(leaf * FRONT + front, moved(leaf, front, k)) for leaf, front in everyone])
        for k in (1, 2, 3)
    ]


def exchange(x, axis, groups=None):
    return lax.all_to_all(x, axis, 0, 0, tiled=True, axis_index_groups=groups)


def body(
    leaf_source,
    top_source,
    leaf_lower_inverse,
    leaf_upper_inverse,
    leaf_lower_block,
    leaf_upper_block,
    top_lower_inverse,
    top_upper_inverse,
    top_lower_block,
    top_upper_block,
    leaf_targets,
    top_targets,
):
    (send,) = call(
        prepare_kernel,
        [((192, SEP), BF)],
        (
            keep(leaf_source),
            keep(top_lower_inverse),
            keep(top_upper_inverse),
            keep(jnp.swapaxes(top_lower_block, 1, 2)),
            keep(top_upper_block),
        ),
        specs=[HBM] * 5,
        scratch=[pltpu.VMEM((PIECE, RHS), F32), pltpu.SemaphoreType.DMA((6,))],
        size=1 << 20,
    )
    early, later = call(
        pack_kernel,
        [((4, 64, SEP), BF), ((4, 128, SEP), BF)],
        (send, *shifts(send, 0)),
        size=1 << 20,
    )
    parts = shifts(early, 1)
    parts[2], leaf_lower_block = lax.optimization_barrier((parts[2], leaf_lower_block))
    spread, hot2, hot3 = call(
        spread_kernel,
        [((SPAN, PIECE), BF), ((SEP, SEP), BF), ((2 * SEP, SEP), BF)],
        (leaf_lower_block, leaf_targets, top_targets),
        flops=2 * UPD * SPAN * PIECE,
        size=2 << 20,
    )
    spread, *parts = lax.optimization_barrier((spread, *parts))
    (ahead,) = call(functools.partial(assemble_kernel, 1), [((SEP, SEP), BF)], (early, *parts), size=1 << 20)
    swapped = swap(ahead, 1)
    solved, send = call(
        leaf_forward_kernel,
        [pltpu.HBM((PIECE, RHS), F32), ((FRONT, 16, HALF), BF)],
        (early, *parts, leaf_lower_inverse, spread, top_source),
        out_specs=[HBM, VMEM],
        scratch=[pltpu.VMEM((SUB, RHS), BF), pltpu.VMEM((PIECE, RHS), F32), pltpu.SemaphoreType.DMA],
        flops=2 * RHS * (PIECE * SUB + UPD * PIECE + UPD * SPAN),
        size=4 << 20,
    )
    parts = shifts(later, 1)
    got = exchange(send, "front")
    got, *parts = lax.optimization_barrier((got, *parts))
    second, later = call(
        assemble_later_kernel, [((SEP, SEP), BF), ((3, SEP, SEP), BF)], (later, *parts), size=4 << 20
    )
    (send,) = call(
        top_forward_kernel,
        [((16, HALF), BF)],
        (got, ahead, swapped, hot3),
        flops=2 * 256 * SEP * SEP * 4,
        size=4 << 20,
    )
    send, second, later = lax.optimization_barrier((send, second, later))
    total, near, other = call(
        group_kernel,
        [((16, HALF), BF), ((16, SEP), BF), ((16, SEP // 2), BF)],
        (send, swap(send, 1), swap(send, 2), swap(send, 3), second, swap(second, 1), hot2),
        flops=2 * 256 * SEP * SEP * 3,
        size=2 << 20,
    )
    near, far, other = swap(near, 4), swap(total, 8), swap(other, 12)
    total, leaf_upper_block = lax.optimization_barrier((total, leaf_upper_block))
    (picked,) = call(
        pick_kernel,
        [((PIECE, SPAN), BF)],
        (leaf_upper_block, leaf_targets),
        flops=2 * UPD * SPAN * PIECE,
        size=2 << 20,
    )
    near, picked = lax.optimization_barrier((near, picked))
    (send,) = call(
        top_backward_kernel,
        [((FRONT, 16, HALF), BF)],
        (total, near, far, other, later, swap(later, 1), hot2, hot3),
        flops=2 * 256 * SEP * SEP * 9,
        size=5 << 20,
    )
    got = exchange(send, "front")
    send, own, side, last = call(
        leaf_backward_kernel,
        [((FRONT, PIECE, RHS), BF), ((96, RHS), F32), ((64, RHS), BF), ((32, RHS), BF)],
        (got, solved, picked),
        specs=[VMEM, HBM, VMEM],
        scratch=[pltpu.VMEM((PIECE, RHS), F32), pltpu.SemaphoreType.DMA],
        flops=2 * RHS * 2 * PIECE * SPAN,
        size=2 << 20,
    )
    near, far, other = swap(last, 4), swap(side, 8), swap(last, 12)
    got = exchange(send, "front")
    leaf_solution, top_solution = call(
        finish_kernel,
        [((1, PIECE, RHS), F32), ((7, ROWS, RHS), F32)],
        (got, leaf_upper_inverse, own, near, far, other),
        flops=2 * RHS * PIECE * SUB,
        size=2 << 20,
    )
    return leaf_solution, top_solution


def solution(mesh):
    in_specs = (
        P("leaf", "front", None),
        P(None, "front", None),
        P("leaf", "front", None),
        P("leaf", "front", None),
        P("leaf", None, "front"),
        P("leaf", "front", None),
        P(None, "front", None),
        P(None, "front", None),
        P(None, None, "front"),
        P(None, "front", None),
        P("leaf", None),
        P(),
    )
    out_specs = (P("leaf", "front", None), P(None, "front", None))
    return jax.shard_map(body, mesh=mesh, in_specs=in_specs, out_specs=out_specs, check_vma=False)
```

```python
import functools

import jax
import jax.numpy as jnp
from jax import lax
from jax.experimental import pallas as pl
from jax.experimental.pallas import tpu as pltpu
from jax.sharding import PartitionSpec as P

BF = jnp.bfloat16
F32 = jnp.float32
FRONT = 16
LEAVES = 16
SUB = 2048
SEP = 512
UPD = 1024
RHS = 128
ROWS = SEP // FRONT
SPAN = 3 * SEP
HALF = SPAN // 2
PIECE = SUB // FRONT
NT = (((1,), (1,)), ((), ()))
NN = (((1,), (0,)), ((), ()))


def dot(a, b, dims):
    return lax.dot_general(a, b, dims, preferred_element_type=F32)


def split_dot(x, w, dims):
    head = x.astype(BF).astype(F32)
    both = jnp.concatenate([head, x - head], axis=0).astype(BF)
    out = dot(both, w, dims)
    return out[:8] + out[8:]


def fold(x):
    half = x.shape[1] // 2
    return jnp.concatenate([x[:, :half], x[:, half:]], axis=0)


def unfold(x):
    return jnp.concatenate([x[:8], x[8:]], axis=1)


def one_hot(first, count, places):
    rows = lax.broadcasted_iota(jnp.int32, (count, places.shape[1]), 0) + first
    return jnp.where(rows == places, 1.0, 0.0).astype(BF)


def leaf_places(targets):
    owner = targets >> 9
    height = jnp.where(owner > 0, 1, 0) + jnp.where(owner > 2, 1, 0)
    return (height << 9) | (targets & (SEP - 1))


def ancestor_places(targets):
    return jnp.where(targets >= SEP, SEP, 0) + (targets & (SEP - 1))


def prepare_kernel(source, low_inv, up_inv, low, up, send, piece, sems):
    leaf = lax.axis_index("leaf")
    third = 3 + (leaf >> 2)
    second = 1 + (leaf >> 3)
    plans = [
        [(low_inv, third), (low_inv, second), (low_inv, 0), (up_inv, 0), (up, second - 1)],
        [(low, third - 1), (low, second - 1), (up_inv, second), (up, third - 1), (up_inv, third)],
    ]
    places = [send.at[pl.ds(i * ROWS + ROWS, ROWS)] for i in range(5)]
    start = pltpu.make_async_copy(source.at[0], piece, sems.at[5])
    start.start()
    for core, plan in enumerate(plans):

        @pl.when((leaf & 1) == core)
        def _(plan=plan):
            copies = [
                pltpu.make_async_copy(ref.at[index], place, sems.at[slot])
                for slot, ((ref, index), place) in enumerate(zip(plan, places))
            ]
            for copy in copies:
                copy.start()
            for copy in copies:
                copy.wait()

    start.wait()
    block = piece[...].astype(BF)
    send[0:ROWS, :] = jnp.concatenate([block[q * ROWS : q * ROWS + ROWS] for q in range(4)], axis=1)


def pack_kernel(own, a, b, c, early, later):
    for k, ref in enumerate((own, a, b, c)):
        early[k] = ref[0:64, :]
        later[k] = ref[64:192, :]


def origin(j, k):
    front = lax.axis_index("front")
    core = lax.axis_index("leaf") & 1
    y, x = front >> 2, front & 3
    dy = jnp.where(core == 0, j, k)
    dx = jnp.where(core == 0, k, j)
    return ((y - dy) & 3) * 4 + ((x - dx) & 3)


def assemble_kernel(skip, own, a, b, c, *outs):
    for j, ref in enumerate((own, a, b, c)):
        for k in range(4):
            rows = pl.ds(pl.multiple_of(origin(j, k) * ROWS, ROWS), ROWS)
            for i, out in enumerate(outs):
                first = (skip + i) * ROWS
                out[rows, :] = ref[k, first : first + ROWS, :]


def assemble_later_kernel(own, a, b, c, second, out):
    assemble_kernel(0, own, a, b, c, second, *[out.at[i] for i in range(3)])


def pick_kernel(block, targets, picked):
    places = leaf_places(targets[...])
    for part in range(3):
        rows = slice(part * SEP, part * SEP + SEP)
        picked[:, rows] = dot(block[0], one_hot(part * SEP, SEP, places), NT).astype(BF)


def spread_kernel(block, targets, top_targets, spread, hot2, hot3):
    leaf = lax.axis_index("leaf")
    hot2[...] = one_hot(0, SEP, top_targets[pl.ds(leaf >> 3, 1), :])
    hot3[...] = one_hot(0, 2 * SEP, ancestor_places(top_targets[pl.ds(2 + (leaf >> 2), 1), :]))
    places = leaf_places(targets[...])
    for part in range(3):
        hot = one_hot(part * SEP, SEP, places)
        spread[part * SEP : part * SEP + SEP, :] = dot(hot, block[0], NN).astype(BF)


def leaf_forward_kernel(own, a, b, c, inverse, spread, top, solved_out, send, source, held, sem):
    leaf = lax.axis_index("leaf")
    front = lax.axis_index("front")
    for j, ref in enumerate((own, a, b, c)):
        for k in range(4):
            at = origin(j, k) * PIECE
            for q in range(4):
                rows = pl.ds(pl.multiple_of(at + q * ROWS, ROWS), ROWS)
                source[rows, :] = ref[k, 0:ROWS, q * RHS : q * RHS + RHS]
    solved = dot(inverse[0], source[...], NN)
    held[...] = solved
    copy = pltpu.make_async_copy(held, solved_out, sem)
    copy.start()
    mine = jnp.concatenate(
        [
            top[0] * (1 / 16),
            top[1 + (leaf >> 3)] * (1 / 8),
            top[3 + (leaf >> 2)] * (1 / 4),
            jnp.zeros((32, RHS), F32),
        ],
        axis=0,
    ).T
    row = lax.broadcasted_iota(jnp.int32, (RHS, SPAN), 0)
    column = lax.broadcasted_iota(jnp.int32, (RHS, SPAN), 1)
    hot = jnp.where(column == ((row >> 5) << 9) + front * ROWS + (row & 31), 1.0, 0.0).astype(BF)
    total = dot(mine.astype(BF), hot, NN) - dot(solved.T.astype(BF), spread[...], NT)
    for to in range(FRONT):
        send[to] = fold(total[to * 8 : to * 8 + 8]).astype(BF)
    copy.wait()


def top_forward_kernel(got, first, swapped, hot3, send):
    leaf = lax.axis_index("leaf")
    total = got[0].astype(F32)
    for k in range(1, FRONT):
        total = total + got[k].astype(F32)
    total = unfold(total)

    def run(even, odd):
        solved3 = split_dot(total[:, 2 * SEP :], even[...], NT)
        update3 = split_dot(solved3, odd[...], NN)
        above = total[:, : 2 * SEP] - split_dot(update3, hot3[...], NT)
        send[...] = fold(jnp.concatenate([above, solved3], axis=1)).astype(BF)

    @pl.when((leaf & 1) == 0)
    def _():
        run(first, swapped)

    @pl.when((leaf & 1) == 1)
    def _():
        run(swapped, first)


def group_kernel(own, a, b, c, first, swapped, hot2, far, near, other):
    core = lax.axis_index("leaf") & 1
    total = (own[...].astype(F32) + a[...].astype(F32)) + (b[...].astype(F32) + c[...].astype(F32))
    total = unfold(total)

    def run(even, odd):
        solved2 = split_dot(total[:, SEP : 2 * SEP], even[...], NT)
        update2 = split_dot(solved2, odd[...], NN)
        target1 = total[:, :SEP] - split_dot(update2, hot2[...], NT)
        far[...] = fold(jnp.concatenate([target1, solved2, total[:, 2 * SEP :]], axis=1)).astype(BF)
        near[...] = fold(jnp.concatenate([target1, solved2], axis=1)).astype(BF)
        other[...] = fold(target1).astype(BF)

    @pl.when(core == 0)
    def _():
        run(first, swapped)

    @pl.when(core == 1)
    def _():
        run(swapped, first)


def top_backward_kernel(own, near, far, other, later, swapped, hot2, hot3, send):
    core = lax.axis_index("leaf") & 1
    part = unfold(own[...].astype(F32))
    side = unfold(near[...].astype(F32))
    total1 = part[:, :SEP] + side[:, :SEP] + unfold(far[...].astype(F32))[:, :SEP] + unfold(other[...].astype(F32))
    total2 = part[:, SEP : 2 * SEP] + side[:, SEP : 2 * SEP]
    total3 = part[:, 2 * SEP :]

    def run(first, last):
        mats = [first[0], first[1], first[2], last[0], last[1], last[2]]
        x1 = split_dot(split_dot(total1, mats[0], NT), mats[1], NT)
        picked2 = split_dot(x1, hot2[...], NN)
        x2 = split_dot(total2 - split_dot(picked2, mats[2], NT), mats[3], NT)
        picked3 = split_dot(jnp.concatenate([x1, x2], axis=1), hot3[...], NN)
        x3 = split_dot(total3 - split_dot(picked3, mats[4], NT), mats[5], NT)
        out = fold(jnp.concatenate([x1, x2, x3], axis=1)).astype(BF)
        for to in range(FRONT):
            send[to] = out

    @pl.when(core == 0)
    def _():
        run(later, swapped)

    @pl.when(core == 1)
    def _():
        run(swapped, later)


def leaf_backward_kernel(got, solved, picked, send, own, side, last, held, sem):
    copy = pltpu.make_async_copy(solved, held, sem)
    copy.start()
    front = lax.axis_index("front")
    full = jnp.concatenate([unfold(got[k].astype(F32)) for k in range(FRONT)], axis=0).astype(BF)
    change = dot(picked[...], full, NT)
    copy.wait()
    residue = (held[...] - change).astype(BF)
    for to in range(FRONT):
        send[to] = residue
    row = lax.broadcasted_iota(jnp.int32, (96, SPAN), 0)
    column = lax.broadcasted_iota(jnp.int32, (96, SPAN), 1)
    pick = jnp.where(column == ((row >> 5) << 9) + front * ROWS + (row & 31), 1.0, 0.0).astype(BF)
    rows = dot(pick, full, NT)
    own[...] = rows
    side[...] = rows[32:96, :].astype(BF)
    last[...] = rows[64:96, :].astype(BF)


def finish_kernel(got, inverse, own, near, far, other, leaf_out, top_out):
    leaf = lax.axis_index("leaf")
    leaf_out[0] = dot(inverse[0], got[...].reshape(SUB, RHS), NN)
    second = leaf >> 3
    third = leaf >> 2
    top_out[0] = own[0:32, :]
    top_out[1 + second] = own[32:64, :]
    top_out[1 + (second ^ 1)] = far[0:32, :].astype(F32)
    top_out[3 + third] = own[64:96, :]
    top_out[3 + (third ^ 1)] = near[...].astype(F32)
    top_out[3 + (third ^ 2)] = far[32:64, :].astype(F32)
    top_out[3 + (third ^ 3)] = other[...].astype(F32)


VMEM = pl.BlockSpec(memory_space=pltpu.VMEM)
HBM = pl.BlockSpec(memory_space=pltpu.HBM)


def keep(x):
    return pltpu.with_memory_space_constraint(x, pltpu.HBM)


def call(kernel, outs, args, specs=None, out_specs=None, scratch=(), flops=0, size=0):
    shapes = [jax.ShapeDtypeStruct(*out) if isinstance(out, tuple) else out for out in outs]
    return pl.pallas_call(
        kernel,
        out_shape=shapes,
        in_specs=specs or [VMEM] * len(args),
        out_specs=out_specs or [VMEM] * len(shapes),
        scratch_shapes=list(scratch),
        compiler_params=pltpu.CompilerParams(vmem_limit_bytes=16 * 1024 * 1024),
        cost_estimate=pl.CostEstimate(flops=flops, bytes_accessed=size, transcendentals=0),
    )(*args)


def swap(x, flip):
    return lax.ppermute(x, "leaf", [(i, i ^ flip) for i in range(LEAVES)])


def shifts(x, turn):
    def moved(leaf, front, k):
        y, x = front // 4, front % 4
        if (leaf + turn) % 2 == 0:
            return leaf * FRONT + y * 4 + (x + k) % 4
        return leaf * FRONT + (y + k) % 4 * 4 + x

    everyone = [(leaf, front) for leaf in range(LEAVES) for front in range(FRONT)]
    return [
        lax.ppermute(x, ("leaf", "front"), [(leaf * FRONT + front, moved(leaf, front, k)) for leaf, front in everyone])
        for k in (1, 2, 3)
    ]


def exchange(x, axis, groups=None):
    return lax.all_to_all(x, axis, 0, 0, tiled=True, axis_index_groups=groups)


def body(
    leaf_source,
    top_source,
    leaf_lower_inverse,
    leaf_upper_inverse,
    leaf_lower_block,
    leaf_upper_block,
    top_lower_inverse,
    top_upper_inverse,
    top_lower_block,
    top_upper_block,
    leaf_targets,
    top_targets,
):
    (send,) = call(
        prepare_kernel,
        [((192, SEP), BF)],
        (
            keep(leaf_source),
            keep(top_lower_inverse),
            keep(top_upper_inverse),
            keep(jnp.swapaxes(top_lower_block, 1, 2)),
            keep(top_upper_block),
        ),
        specs=[HBM] * 5,
        scratch=[pltpu.VMEM((PIECE, RHS), F32), pltpu.SemaphoreType.DMA((6,))],
        size=1 << 20,
    )
    early, later = call(
        pack_kernel,
        [((4, 64, SEP), BF), ((4, 128, SEP), BF)],
        (send, *shifts(send, 0)),
        size=1 << 20,
    )
    parts = shifts(early, 1)
    parts[2], leaf_lower_block = lax.optimization_barrier((parts[2], leaf_lower_block))
    spread, hot2, hot3 = call(
        spread_kernel,
        [((SPAN, PIECE), BF), ((SEP, SEP), BF), ((2 * SEP, SEP), BF)],
        (leaf_lower_block, leaf_targets, top_targets),
        flops=2 * UPD * SPAN * PIECE,
        size=2 << 20,
    )
    spread, *parts = lax.optimization_barrier((spread, *parts))
    (ahead,) = call(functools.partial(assemble_kernel, 1), [((SEP, SEP), BF)], (early, *parts), size=1 << 20)
    swapped = swap(ahead, 1)
    solved, send = call(
        leaf_forward_kernel,
        [pltpu.HBM((PIECE, RHS), F32), ((FRONT, 16, HALF), BF)],
        (early, *parts, leaf_lower_inverse, spread, top_source),
        out_specs=[HBM, VMEM],
        scratch=[pltpu.VMEM((SUB, RHS), BF), pltpu.VMEM((PIECE, RHS), F32), pltpu.SemaphoreType.DMA],
        flops=2 * RHS * (PIECE * SUB + UPD * PIECE + UPD * SPAN),
        size=4 << 20,
    )
    parts = shifts(later, 1)
    got = exchange(send, "front")
    got, *parts = lax.optimization_barrier((got, *parts))
    second, later = call(
        assemble_later_kernel, [((SEP, SEP), BF), ((3, SEP, SEP), BF)], (later, *parts), size=4 << 20
    )
    (send,) = call(
        top_forward_kernel,
        [((16, HALF), BF)],
        (got, ahead, swapped, hot3),
        flops=2 * 256 * SEP * SEP * 4,
        size=4 << 20,
    )
    send, second = lax.optimization_barrier((send, second))
    total, near, other = call(
        group_kernel,
        [((16, HALF), BF), ((16, SEP), BF), ((16, SEP // 2), BF)],
        (send, swap(send, 1), swap(send, 2), swap(send, 3), second, swap(second, 1), hot2),
        flops=2 * 256 * SEP * SEP * 3,
        size=2 << 20,
    )
    near, far, other = swap(near, 4), swap(total, 8), swap(other, 12)
    total, later, leaf_upper_block = lax.optimization_barrier((total, later, leaf_upper_block))
    (picked,) = call(
        pick_kernel,
        [((PIECE, SPAN), BF)],
        (leaf_upper_block, leaf_targets),
        flops=2 * UPD * SPAN * PIECE,
        size=2 << 20,
    )
    near, picked = lax.optimization_barrier((near, picked))
    (send,) = call(
        top_backward_kernel,
        [((FRONT, 16, HALF), BF)],
        (total, near, far, other, later, swap(later, 1), hot2, hot3),
        flops=2 * 256 * SEP * SEP * 9,
        size=5 << 20,
    )
    got = exchange(send, "front")
    send, own, side, last = call(
        leaf_backward_kernel,
        [((FRONT, PIECE, RHS), BF), ((96, RHS), F32), ((64, RHS), BF), ((32, RHS), BF)],
        (got, solved, picked),
        specs=[VMEM, HBM, VMEM],
        scratch=[pltpu.VMEM((PIECE, RHS), F32), pltpu.SemaphoreType.DMA],
        flops=2 * RHS * 2 * PIECE * SPAN,
        size=2 << 20,
    )
    near, far, other = swap(last, 4), swap(side, 8), swap(last, 12)
    got = exchange(send, "front")
    leaf_solution, top_solution = call(
        finish_kernel,
        [((1, PIECE, RHS), F32), ((7, ROWS, RHS), F32)],
        (got, leaf_upper_inverse, own, near, far, other),
        flops=2 * RHS * PIECE * SUB,
        size=2 << 20,
    )
    return leaf_solution, top_solution


def solution(mesh):
    in_specs = (
        P("leaf", "front", None),
        P(None, "front", None),
        P("leaf", "front", None),
        P("leaf", "front", None),
        P("leaf", None, "front"),
        P("leaf", "front", None),
        P(None, "front", None),
        P(None, "front", None),
        P(None, None, "front"),
        P(None, "front", None),
        P("leaf", None),
        P(),
    )
    out_specs = (P("leaf", "front", None), P(None, "front", None))
    return jax.shard_map(body, mesh=mesh, in_specs=in_specs, out_specs=out_specs, check_vma=False)
```
